32 devices in a mesh: seq: 32 (over z, y, x, core).
Axes of the slice: x: 2, y: 2, z: 4, core: 2. Of those that a mesh axis runs over, the one named last changes fastest.
Arguments:
- tokens: bfloat16 [16384, 192], P('seq'), may hold values from -6 to 6
- out_grad: bfloat16 [16384, 192], P('seq'), may hold values from -6 to 6
- spread_weight: bfloat16 [384, 768], replicated, may hold values from -0.3125 to 0.3125
- merge_weight: bfloat16 [768, 384], replicated, may hold values from -0.21875 to 0.21875
- switch_bias: float32 [384], replicated, may hold values from -4 to 4
- gate_logit: float32 [384], replicated, may hold values from -1 to 3
Outputs:
- network_out: bfloat16 [16384, 192], P('seq')
- token_grad: bfloat16 [16384, 192], P('seq')
- spread_grad: float32 [384, 768], replicated
- merge_grad: float32 [768, 384], replicated
- bias_grad: float32 [384], replicated
- gate_grad: float32 [384], replicated
The draws below stay inside these ranges and needn't reach their ends.
All inputs are finite; a program needn't handle non-finite values.
Results may differ from the reference program's by a relative error of at most 0.008.
Values may be sent and summed in bfloat16 or wider, within the bound.
A program may use at most 64 MiB of HBM per device.

```python
import math
import jax
import jax.numpy as jnp
from jax import lax

D = 192
SWITCH = 384
HIDDEN_SIZE = 768
ROWS_DEV = 512
SECTIONS = 4
TOKENS = 16384
N_SEQ = 32


def level_of(key, dims, shards, smallest, largest):
    def one(axis_at, blocks):
        draws = jax.random.uniform(jax.random.fold_in(jax.random.fold_in(key, 6), axis_at), (blocks,), jnp.float32, smallest / len(shards), largest / len(shards))
        return jnp.repeat(jnp.exp(draws), dims[axis_at] // blocks).reshape((-1,) + (1,) * (len(dims) - axis_at - 1))

    factor_of = one(*shards[0])
    for cut in shards[1:]:
        factor_of = factor_of * one(*cut)
    return factor_of


def noise(stream_key, extent, scale, reach, shards=(), held_as=jnp.bfloat16):
    factor_of = level_of(stream_key, extent, shards, -0.22, 0.18) if shards else 1.0
    result = jax.random.normal(stream_key, extent, jnp.float32) * scale * factor_of
    return jnp.minimum(jnp.maximum(result, -reach), reach).astype(held_as)


def setup_inputs(seed: int = 0) -> dict:
    arg_keys = jax.random.split(jax.random.key(seed), 7)
    return {
        "tokens": noise(arg_keys[0], (TOKENS, D), 1.0, 6.0, ((0, 32),)),
        "out_grad": noise(arg_keys[1], (TOKENS, D), 1.0, 6.0, ((0, 32),)),
        "spread_weight": noise(arg_keys[2], (SWITCH, HIDDEN_SIZE), SWITCH ** -0.5, 0.3125),
        "merge_weight": noise(arg_keys[3], (HIDDEN_SIZE, SWITCH), HIDDEN_SIZE ** -0.5, 0.21875),
        "switch_bias": noise(arg_keys[4], (SWITCH,), 1.0, 4.0, (), jnp.float32),
        "gate_logit": jnp.clip(jax.random.uniform(arg_keys[5], (SWITCH,), jnp.float32, -1.0, 3.0), -1.0, 3.0),
    }


sqrt_half = 0.7071067811865476
inv_sqrt_two_pi = 0.3989422804014327

def gelu_exact(values):
    return 0.5 * values * (1.0 + lax.erf(values * sqrt_half))

def gelu_slope(values):
    return 0.5 * (1.0 + lax.erf(values * sqrt_half)) + values * jnp.exp(-0.5 * values * values) * inv_sqrt_two_pi

def normalize(pre_norm):
    centered = pre_norm - lax.optimization_barrier(jnp.mean(pre_norm, -1, keepdims=True))
    inv_scale = lax.rsqrt(lax.optimization_barrier(jnp.mean(centered * centered, -1, keepdims=True)) + 1e-05)
    return (centered * inv_scale, inv_scale)

def switch_forward(paired, spread_weight, merge_weight, switch_bias, gate_logit):
    pre_norm = jnp.dot(paired, spread_weight, preferred_element_type=jnp.float32)
    normed, inv_scale = normalize(pre_norm)
    hidden = gelu_exact(normed).astype(jnp.bfloat16)
    branch = jnp.dot(hidden, merge_weight, preferred_element_type=jnp.float32) + switch_bias
    return (jax.nn.sigmoid(gate_logit) * paired.astype(jnp.float32) + 0.25 * branch).astype(jnp.bfloat16)

def switch_backward(paired, grad_pairs, spread_weight, merge_weight, gate_logit):
    pre_norm = jnp.dot(paired, spread_weight, preferred_element_type=jnp.float32)
    normed, inv_scale = normalize(pre_norm)
    hidden = gelu_exact(normed).astype(jnp.bfloat16)
    grad_rows = grad_pairs.astype(jnp.float32)
    gate_term = lax.optimization_barrier(jnp.sum(grad_rows * paired.astype(jnp.float32), 0))
    bias_term = 0.25 * lax.optimization_barrier(jnp.sum(grad_rows, 0))
    branch_grad = (0.25 * grad_rows).astype(jnp.bfloat16)
    merge_term = lax.dot_general(hidden, branch_grad, (((0,), (0,)), ((), ())), preferred_element_type=jnp.float32)
    hidden_grad = lax.dot_general(branch_grad, merge_weight, (((1,), (1,)), ((), ())), preferred_element_type=jnp.float32)
    normed_grad = hidden_grad * gelu_slope(normed)
    pre_grad = inv_scale * (normed_grad - lax.optimization_barrier(jnp.mean(normed_grad, -1, keepdims=True)) - normed * lax.optimization_barrier(jnp.mean(normed_grad * normed, -1, keepdims=True)))
    pre_grad = pre_grad.astype(jnp.bfloat16)
    spread_term = lax.dot_general(paired, pre_grad, (((0,), (0,)), ((), ())), preferred_element_type=jnp.float32)
    back_rows = lax.dot_general(pre_grad, spread_weight, (((1,), (1,)), ((), ())), preferred_element_type=jnp.float32)
    paired_grad = (jax.nn.sigmoid(gate_logit) * grad_rows + back_rows).astype(jnp.bfloat16)
    return (paired_grad, (spread_term, merge_term, bias_term, gate_term))

def to_pairs(rows, distance):
    viewed = rows.reshape(rows.shape[0] // (2 * distance), 2, distance, rows.shape[1])
    return jnp.concatenate([viewed[:, 0], viewed[:, 1]], -1).reshape(-1, 2 * rows.shape[1])

def from_pairs(paired, distance):
    unit_count = paired.shape[1] // 2
    viewed = paired.reshape(-1, distance, 2 * unit_count)
    return jnp.stack([viewed[..., :unit_count], viewed[..., unit_count:]], 1).reshape(-1, unit_count)

def reference(tokens, out_grad, spread_weight, merge_weight, switch_bias, gate_logit):
    device_bits = N_SEQ.bit_length() - 1
    pair_count = TOKENS // 2
    block_rows = math.gcd(pair_count, 8192)
    block_count = pair_count // block_rows
    current = tokens
    saved = []
    for section_num in range(SECTIONS):
        distance = ROWS_DEV * 2 ** (device_bits - 1 - section_num)
        paired = to_pairs(current, distance)
        saved.append(paired)
        blocks = paired.reshape(block_count, block_rows, -1)
        switched = lax.map(lambda block: switch_forward(block, spread_weight, merge_weight, switch_bias, gate_logit), blocks)
        current = from_pairs(switched.reshape(pair_count, -1), distance)
    network_out = current
    grad_rows = out_grad
    spread_total = jnp.zeros(spread_weight.shape, jnp.float32)
    merge_total = jnp.zeros(merge_weight.shape, jnp.float32)
    bias_total = jnp.zeros(switch_bias.shape, jnp.float32)
    gate_total = jnp.zeros(gate_logit.shape, jnp.float32)
    for section_num in reversed(range(SECTIONS)):
        distance = ROWS_DEV * 2 ** (device_bits - 1 - section_num)
        grad_pairs = to_pairs(grad_rows, distance)
        pair_blocks = saved[section_num].reshape(block_count, block_rows, -1)
        grad_blocks = grad_pairs.reshape(block_count, block_rows, -1)
        paired_grad, term_list = lax.map(lambda both: switch_backward(both[0], both[1], spread_weight, merge_weight, gate_logit), (pair_blocks, grad_blocks))
        spread_total = spread_total + lax.optimization_barrier(jnp.sum(term_list[0], 0))
        merge_total = merge_total + lax.optimization_barrier(jnp.sum(term_list[1], 0))
        bias_total = bias_total + lax.optimization_barrier(jnp.sum(term_list[2], 0))
        gate_total = gate_total + lax.optimization_barrier(jnp.sum(term_list[3], 0))
        grad_rows = from_pairs(paired_grad.reshape(pair_count, -1), distance)
    grad_scale = 1.0 / math.sqrt(TOKENS)
    gate_open = jax.nn.sigmoid(gate_logit)
    return (network_out, grad_rows, spread_total * grad_scale, merge_total * grad_scale, bias_total * grad_scale, gate_total * gate_open * (1.0 - gate_open) * grad_scale)
```

```python
import functools
import math

import jax
import jax.numpy as jnp
from jax import lax
from jax.experimental import pallas as pl
from jax.experimental.pallas import tpu as pltpu
from jax.sharding import PartitionSpec as P

SECTIONS = 4
GROUP = 2**SECTIONS
SIDE = 4
LANES = 128
MESH = pl.DeviceIdType.MESH
F32 = jnp.float32
BF16 = jnp.bfloat16

sqrt_half = 0.7071067811865476
inv_sqrt_two_pi = 0.3989422804014327


def dot(a, b):
    return jnp.dot(a, b, preferred_element_type=F32)


def rounded_up(size):
    return -(-size // LANES) * LANES


def step_kernel(
    n,
    tok, og, sw, mw, bias, gate,
    net_o, tg_o, res, vec_o,
    sw_v, mw_v, bias_v, gate_v,
    xin, gin, xs, gs,
    state, wp, wt, mp, mt, rows_v,
    sides, wides, r_sides, r_wides,
    pre, normed, slope, inv,
    flat, flat_b, part, part_b, rv1, rv2, rvx, last,
    sums, v0, v1, v2, v3, rvm, rvv1, rvv2, rvvx,
    load_sem, a2a_sem, mate_sem, rs1_sem, rs2_sem, rsx_sem, ag1_sem, ag2_sem, fwd_sem,
    vm_sem, vv1_sem, vv2_sem, vvx_sem,
):
    rows, units = xin.shape
    sub = rows // GROUP
    half = rows // 2
    hidden_size = sw_v.shape[1]
    stride = n // GROUP
    others = n // (2 * GROUP)
    quarter = flat.shape[0] // SIDE
    piece = quarter // SIDE

    me = lax.axis_index("seq")
    top = me // stride
    low = me % stride
    core = me % 2
    mid = low // 2
    mate = me + 1 - 2 * core
    col = top % SIDE
    line = top // SIDE

    def dev(which):
        return which * stride + low

    def mid_dev(which):
        return top * stride + which * 2 + core

    def remote(src, dst, sems, target):
        return pltpu.make_async_remote_copy(
            src_ref=src, dst_ref=dst, send_sem=sems.at[0], recv_sem=sems.at[1],
            device_id=(target,), device_id_type=MESH,
        )

    loads = [
        pltpu.make_async_copy(tok.at[pl.ds(top * sub, sub)], xin.at[pl.ds(top * sub, sub)], load_sem.at[0]),
        pltpu.make_async_copy(og.at[pl.ds(top * sub, sub)], gin.at[pl.ds(top * sub, sub)], load_sem.at[1]),
        pltpu.make_async_copy(sw, sw_v, load_sem.at[2]),
        pltpu.make_async_copy(mw, mw_v, load_sem.at[3]),
        pltpu.make_async_copy(bias, bias_v, load_sem.at[4]),
        pltpu.make_async_copy(gate, gate_v, load_sem.at[5]),
    ]
    for load in loads:
        load.start()

    barrier = pltpu.get_barrier_semaphore()

    @pl.loop(1, GROUP)
    def _(j):
        pl.semaphore_signal(barrier, inc=1, device_id=(dev((top + j) % GROUP),), device_id_type=MESH)

    pl.semaphore_signal(barrier, inc=1, device_id=(mate,), device_id_type=MESH)
    for j in range(1, others):
        pl.semaphore_signal(
            barrier, inc=1, device_id=(mid_dev((mid + j) % others),), device_id_type=MESH
        )
    pl.semaphore_wait(barrier, GROUP + others - 1)

    def exchange(src, dst, number):
        def one(j):
            to = (top + j) % GROUP
            return remote(
                src.at[pl.ds(to * sub, sub)], dst.at[pl.ds(top * sub, sub)],
                a2a_sem.at[number, j], dev(to),
            )

        def start():
            @pl.loop(1, GROUP)
            def _(j):
                one(j).start()

        def received():
            @pl.loop(1, GROUP)
            def _(j):
                one(j).wait_recv()

        def sent():
            @pl.loop(1, GROUP)
            def _(j):
                one(j).wait_send()

        return start, received, sent

    tok_start, tok_received, tok_sent = exchange(tok, xin, 0)
    og_start, og_received, og_sent = exchange(og, gin, 1)
    net_start, net_received, net_sent = exchange(xs, net_o, 2)
    tg_start, tg_received, tg_sent = exchange(gs, tg_o, 3)
    tok_start()
    og_start()

    pad = wp.shape[1] - units
    loads[2].wait()
    loads[3].wait()
    turned = mw_v[...].T
    for h in range(2):
        wp[h, :units] = sw_v[h * units : (h + 1) * units]
        wp[h, units:] = jnp.zeros((pad, hidden_size), BF16)
        wt[h] = wp[h].T
        mt[h, :units] = turned[h * units : (h + 1) * units]
        mt[h, units:] = jnp.zeros((pad, hidden_size), BF16)
        mp[h] = mt[h].T
    loads[4].wait()
    loads[5].wait()
    rows_v[...] = jnp.zeros(rows_v.shape, F32)
    for h in range(2):
        rows_v[h : h + 1, :units] = jax.nn.sigmoid(gate_v[:, h * units : (h + 1) * units])
        rows_v[2 + h : 3 + h, :units] = bias_v[:, h * units : (h + 1) * units]
    sums[...] = jnp.zeros(sums.shape, F32)
    state[...] = jnp.zeros(state.shape, BF16)

    def spans(section):
        length = half >> section
        for k in range(2**section):
            for h in range(2):
                at = (2 * k + h) * length
                yield h, slice(k * length, (k + 1) * length), slice(at, at + length)

    chunk = 32
    loads[0].wait()
    tok_received()
    state[:, :units] = xin[...]
    for s in range(SECTIONS):
        for h, inner, outer in spans(s):
            sides[1, s, h, inner] = state[outer]
        pre[...] = dot(sides[1, s, 0], wp[0]) + dot(sides[1, s, 1], wp[1])

        @pl.loop(0, half // chunk)
        def _(i):
            at = pl.ds(pl.multiple_of(i * chunk, chunk), chunk)
            value = pre[at]
            centered = value - jnp.mean(value, -1, keepdims=True)
            scale = lax.rsqrt(jnp.mean(centered * centered, -1, keepdims=True) + 1e-05)
            value = centered * scale
            phi_sum = 0.5 * (1.0 + lax.erf(value * sqrt_half))
            wides[0, s, at] = (value * phi_sum).astype(BF16)
            normed[s, at] = value
            slope[s, at] = phi_sum + value * jnp.exp(-0.5 * value * value) * inv_sqrt_two_pi
            inv[s, at] = jnp.broadcast_to(scale, (chunk, LANES))

        outs = [
            (
                rows_v[h : h + 1] * sides[1, s, h].astype(F32)
                + 0.25 * (dot(wides[0, s], mp[h]) + rows_v[2 + h : 3 + h])
            ).astype(BF16)
            for h in range(2)
        ]
        for h, inner, outer in spans(s):
            if s < SECTIONS - 1:
                state[outer] = outs[h][inner]
            else:
                xs[outer] = outs[h][inner, :units]
    net_start()
    net_o[pl.ds(top * sub, sub)] = xs[pl.ds(top * sub, sub)]

    def gather_grads(side, wide, first):
        for h in range(2):
            term = dot(side[h].T[:units], wide[...])
            for c in range(hidden_size // LANES):
                at = slice((2 * c + h) * units, (2 * c + h + 1) * units)
                block = term[:, c * LANES : (c + 1) * LANES]
                flat[at] = block if first else flat[at] + block

    def mate_copies(s):
        return [
            remote(sides.at[1 - core, s], r_sides.at[s], mate_sem.at[0, s], mate),
            remote(wides.at[1 - core, s], r_wides.at[s], mate_sem.at[1, s], mate),
        ]

    vec_mate = remote(v0, rvm, vm_sem, mate)
    loads[1].wait()
    og_received()
    state[:, :units] = gin[...]
    for s in reversed(range(SECTIONS)):
        grads = [None, None]
        for h, inner, outer in spans(s):
            sides[0, s, h, inner] = (0.25 * state[outer].astype(F32)).astype(BF16)
        pre[...] = dot(sides[0, s, 0], mt[0]) + dot(sides[0, s, 1], mt[1])
        for h in range(2):
            value = 4.0 * sides[0, s, h].astype(F32)
            gated = value * sides[1, s, h].astype(F32)
            sums[h] += jnp.sum(value.reshape(-1, 8, value.shape[1]), 0)
            sums[2 + h] += jnp.sum(gated.reshape(-1, 8, value.shape[1]), 0)
        if s == 0:
            for r in range(4):
                v0[r : r + 1] = jnp.sum(sums[r], 0, keepdims=True)
            vec_mate.start()

        @pl.loop(0, half // chunk)
        def _(i):
            at = pl.ds(pl.multiple_of(i * chunk, chunk), chunk)
            value = normed[s, at]
            grad = pre[at] * slope[s, at]
            grad = (
                grad
                - jnp.mean(grad, -1, keepdims=True)
                - value * jnp.mean(grad * value, -1, keepdims=True)
            ) * inv[s, at][:, :1]
            wides[1, s, at] = grad.astype(BF16)

        for copy in mate_copies(s):
            copy.start()
        for h in range(2):
            back = dot(wides[1, s], wt[h])
            grads[h] = back
        for h, inner, outer in spans(s):
            value = (
                rows_v[h : h + 1] * (state[outer].astype(F32)) + grads[h][inner]
            ).astype(BF16)
            if s > 0:
                state[outer] = value
            else:
                gs[outer] = value[:, :units]
        if s == 0:
            tg_start()
            tg_o[pl.ds(top * sub, sub)] = gs[pl.ds(top * sub, sub)]
        gather_grads(sides.at[core, s], wides.at[core, s], s == SECTIONS - 1)
        if s < SECTIONS - 1:
            for copy in mate_copies(s + 1):
                copy.wait_recv()
            gather_grads(r_sides.at[s + 1], r_wides.at[s + 1], False)
    for copy in mate_copies(0):
        copy.wait_recv()
    gather_grads(r_sides.at[0], r_wides.at[0], False)
    flat_b[...] = flat[...].astype(BF16)

    def first_copies(j):
        to = (col + j) % SIDE
        target = dev(line * SIDE + to)
        return [
            remote(flat_b.at[pl.ds(to * quarter, quarter)], rv1.at[j - 1], rs1_sem.at[j], target),
            remote(v1, rvv1.at[j - 1], vv1_sem.at[j], target),
        ]

    def second_copies(j):
        to = (line + j) % SIDE
        target = dev(to * SIDE + col)
        return [
            remote(part_b.at[pl.ds(to * piece, piece)], rv2.at[j - 1], rs2_sem.at[j], target),
            remote(v2, rvv2.at[j - 1], vv2_sem.at[j], target),
        ]

    def other_copies(j):
        target = mid_dev((mid + j) % others)
        return [
            remote(last, rvx.at[j - 1], rsx_sem.at[j], target),
            remote(v3, rvvx.at[j - 1], vvx_sem.at[j], target),
        ]

    for j in range(1, SIDE):
        first_copies(j)[0].start()
    vec_mate.wait_recv()
    v1[...] = v0[...] + rvm[...]
    for j in range(1, SIDE):
        first_copies(j)[1].start()
    for j in range(1, SIDE):
        for copy in first_copies(j):
            copy.wait_recv()
    total = flat[pl.ds(pl.multiple_of(col * quarter, quarter), quarter)]
    for j in range(SIDE - 1):
        total = total + rv1[j].astype(F32)
    part[...] = total
    part_b[...] = total.astype(BF16)
    v2[...] = v1[...] + rvv1[0] + rvv1[1] + rvv1[2]
    for j in range(1, SIDE):
        for copy in second_copies(j):
            copy.start()
    for j in range(1, SIDE):
        for copy in second_copies(j):
            copy.wait_recv()
    total = part[pl.ds(pl.multiple_of(line * piece, piece), piece)]
    for j in range(SIDE - 1):
        total = total + rv2[j].astype(F32)
    vec = v2[...] + rvv2[0] + rvv2[1] + rvv2[2]
    if others > 1:
        last[...] = total.astype(BF16)
        v3[...] = vec
        for j in range(1, others):
            for copy in other_copies(j):
                copy.start()
        for j in range(1, others):
            for copy in other_copies(j):
                copy.wait_recv()
            total = total + rvx[j - 1].astype(F32)
            vec = vec + rvvx[j - 1]
    vec_o[...] = vec
    mine = pl.ds(pl.multiple_of(col * quarter + line * piece, piece), piece)
    res[core, mine] = total.astype(BF16)

    def line_copy(j):
        to = (line + j) % SIDE
        return remote(res.at[core, mine], res.at[core, mine], ag2_sem.at[j], dev(to * SIDE + col))

    whole = pl.ds(pl.multiple_of(col * quarter, quarter), quarter)

    def col_copy(j):
        to = (col + j) % SIDE
        return remote(res.at[core, whole], res.at[core, whole], ag1_sem.at[j], dev(line * SIDE + to))

    def mate_copy(j):
        at = (col + SIDE - j) % SIDE
        span = res.at[core, pl.ds(pl.multiple_of(at * quarter, quarter), quarter)]
        return remote(span, span, fwd_sem.at[j], mate)

    for j in range(1, SIDE):
        line_copy(j).start()
    for j in range(1, SIDE):
        line_copy(j).wait_recv()
    for j in range(1, SIDE):
        col_copy(j).start()
    mate_copy(0).start()
    for j in range(1, SIDE):
        col_copy(j).wait_recv()
        mate_copy(j).start()

    tok_sent()
    og_sent()
    net_sent()
    tg_sent()
    for s in range(SECTIONS):
        for copy in mate_copies(s):
            copy.wait_send()
    vec_mate.wait_send()
    for j in range(1, SIDE):
        for copy in first_copies(j) + second_copies(j) + [line_copy(j), col_copy(j)]:
            copy.wait_send()
    for j in range(1, others):
        for copy in other_copies(j):
            copy.wait_send()
    net_received()
    tg_received()
    for j in range(SIDE):
        mate_copy(j).wait()


def finish_kernel(scale, res, net, tg, vec, gate, net_o, tg_o, spread_o, merge_o, bias_o, gate_o):
    units = net.shape[1]
    tall, wide = spread_o.shape
    net_o[...] = net[...]
    tg_o[...] = tg[...]
    for c in range(wide // LANES):
        across = slice(c * LANES, (c + 1) * LANES)
        spread_o[:, across] = res[1, c * tall : (c + 1) * tall].astype(F32) * scale
        for k in range(tall // LANES):
            at = c * tall + k * LANES
            merge_o[across, k * LANES : (k + 1) * LANES] = (
                res[0, at : at + LANES].astype(F32) * scale
            ).T
    opened = jax.nn.sigmoid(gate[...])
    opened = opened * (1.0 - opened) * scale
    for h in range(2):
        at = slice(h * units, (h + 1) * units)
        bias_o[:, at] = vec[h : h + 1, :units] * (0.25 * scale)
        gate_o[:, at] = vec[2 + h : 3 + h, :units] * opened[:, at]


def on_device(tokens, out_grad, spread_weight, merge_weight, switch_bias, gate_logit):
    n = lax.axis_size("seq")
    rows, units = tokens.shape
    switch, hidden_size = spread_weight.shape
    half = rows // 2
    wide_units = rounded_up(units)
    others = n // (2 * GROUP)
    more = max(others - 1, 1)
    flat_rows = switch * hidden_size // LANES
    quarter = flat_rows // SIDE
    piece = quarter // SIDE
    vec_shape = (4, wide_units)
    any_spec = pl.BlockSpec(memory_space=pl.ANY)
    vmem_spec = pl.BlockSpec(memory_space=pltpu.VMEM)
    dma = pltpu.SemaphoreType.DMA
    vmem = pltpu.VMEM
    gate_row = gate_logit.reshape(1, switch)
    net, tg, res, vec = pl.pallas_call(
        functools.partial(step_kernel, n),
        out_shape=(
            jax.ShapeDtypeStruct((rows, units), BF16),
            jax.ShapeDtypeStruct((rows, units), BF16),
            jax.ShapeDtypeStruct((2, flat_rows, LANES), BF16),
            jax.ShapeDtypeStruct(vec_shape, F32),
        ),
        in_specs=[any_spec] * 6,
        out_specs=(vmem_spec,) * 4,
        scratch_shapes=[
            vmem((switch, hidden_size), BF16),
            vmem((hidden_size, switch), BF16),
            vmem((1, switch), F32),
            vmem((1, switch), F32),
            vmem((rows, units), BF16),
            vmem((rows, units), BF16),
            vmem((rows, units), BF16),
            vmem((rows, units), BF16),
            vmem((rows, wide_units), BF16),
            vmem((2, wide_units, hidden_size), BF16),
            vmem((2, hidden_size, wide_units), BF16),
            vmem((2, hidden_size, wide_units), BF16),
            vmem((2, wide_units, hidden_size), BF16),
            vmem((8, wide_units), F32),
            vmem((2, SECTIONS, 2, half, wide_units), BF16),
            vmem((2, SECTIONS, half, hidden_size), BF16),
            vmem((SECTIONS, 2, half, wide_units), BF16),
            vmem((SECTIONS, half, hidden_size), BF16),
            vmem((half, hidden_size), F32),
            vmem((SECTIONS, half, hidden_size), F32),
            vmem((SECTIONS, half, hidden_size), F32),
            vmem((SECTIONS, half, LANES), F32),
            vmem((flat_rows, LANES), F32),
            vmem((flat_rows, LANES), BF16),
            vmem((quarter, LANES), F32),
            vmem((quarter, LANES), BF16),
            vmem((SIDE - 1, quarter, LANES), BF16),
            vmem((SIDE - 1, piece, LANES), BF16),
            vmem((more, piece, LANES), BF16),
            vmem((piece, LANES), BF16),
            vmem((4, 8, wide_units), F32),
            vmem(vec_shape, F32),
            vmem(vec_shape, F32),
            vmem(vec_shape, F32),
            vmem(vec_shape, F32),
            vmem(vec_shape, F32),
            vmem((SIDE - 1,) + vec_shape, F32),
            vmem((SIDE - 1,) + vec_shape, F32),
            vmem((more,) + vec_shape, F32),
            dma((6,)),
            dma((4, GROUP, 2)),
            dma((2, SECTIONS, 2)),
            dma((SIDE, 2)),
            dma((SIDE, 2)),
            dma((more + 1, 2)),
            dma((SIDE, 2)),
            dma((SIDE, 2)),
            dma((SIDE, 2)),
            dma((2,)),
            dma((SIDE, 2)),
            dma((SIDE, 2)),
            dma((more + 1, 2)),
        ],
        compiler_params=pltpu.CompilerParams(
            collective_id=0, has_side_effects=True, vmem_limit_bytes=48 * 2**20
        ),
        name="switch_step",
    )(tokens, out_grad, spread_weight, merge_weight, switch_bias.reshape(1, switch), gate_row)
    scale = 1.0 / math.sqrt(n * rows)
    net, tg, spread, merge, bias, gate = pl.pallas_call(
        functools.partial(finish_kernel, scale),
        out_shape=(
            jax.ShapeDtypeStruct((rows, units), BF16),
            jax.ShapeDtypeStruct((rows, units), BF16),
            jax.ShapeDtypeStruct((switch, hidden_size), F32),
            jax.ShapeDtypeStruct((hidden_size, switch), F32),
            jax.ShapeDtypeStruct((1, switch), F32),
            jax.ShapeDtypeStruct((1, switch), F32),
        ),
        in_specs=[vmem_spec] * 5,
        out_specs=(vmem_spec,) * 6,
        compiler_params=pltpu.CompilerParams(vmem_limit_bytes=32 * 2**20),
        name="finish",
    )(res, net, tg, vec, gate_row)
    return net, tg, spread, merge, bias.reshape(switch), gate.reshape(switch)


def solution(mesh):
    placed = (P("seq", None), P("seq", None), P(), P(), P(), P())
    return jax.shard_map(
        on_device,
        mesh=mesh,
        in_specs=placed,
        out_specs=placed,
        check_vma=False,
    )
```

```python
import functools
import math

import jax
import jax.numpy as jnp
from jax import lax
from jax.experimental import pallas as pl
from jax.experimental.pallas import tpu as pltpu
from jax.sharding import PartitionSpec as P

SECTIONS = 4
GROUP = 2**SECTIONS
SIDE = 4
LANES = 128
MESH = pl.DeviceIdType.MESH
F32 = jnp.float32
BF16 = jnp.bfloat16

log2_e = 1.4426950408889634
inv_sqrt_two_pi = 0.3989422804014327


def dot(a, b):
    return jnp.dot(a, b, preferred_element_type=F32)


def distribution(value, bell):
    base = 1.0 + (0.3275911 * 0.7071067811865476) * jnp.abs(value)
    guess = pl.reciprocal(base, approx=True)
    t = guess * (2.0 - base * guess)
    tail = 0.5 * 1.061405429
    for factor in (-1.453152027, 1.421413741, -0.284496736, 0.254829592):
        tail = tail * t + 0.5 * factor
    tail = tail * t * bell
    return jnp.where(value < 0.0, tail, 1.0 - tail)


def rounded_up(size):
    return -(-size // LANES) * LANES


def step_kernel(
    n,
    tok, og, sw, mw, bias, gate,
    net_o, tg_o, res, vec_o,
    sw_v, mw_v, bias_v, gate_v,
    xt, gt, tok_v, og_v, xin, gin, xs, gs,
    state, wp, wt, mp, mt, rows_v,
    sides, wides, r_sides, r_wides,
    pre, normed, slope, inv,
    flat, flat_b, part, part_b, rv1, rv2, rvx, last,
    sums, v0, v1, v2, v3, rvm, rvv1, rvv2, rvvx,
    load_sem, a2a_sem, mate_sem, rs1_sem, rs2_sem, rsx_sem, ag1_sem, ag2_sem, fwd_sem,
    vm_sem, vv1_sem, vv2_sem, vvx_sem,
):
    rows, units = xin.shape
    sub = rows // GROUP
    half = rows // 2
    hidden_size = sw_v.shape[1]
    stride = n // GROUP
    others = n // (2 * GROUP)
    quarter = flat.shape[0] // SIDE
    piece = quarter // SIDE

    me = lax.axis_index("seq")
    top = me // stride
    low = me % stride
    core = me % 2
    mid = low // 2
    mate = me + 1 - 2 * core
    col = top % SIDE
    line = top // SIDE

    def dev(which):
        return which * stride + low

    def mid_dev(which):
        return top * stride + which * 2 + core

    def remote(src, dst, sems, target):
        return pltpu.make_async_remote_copy(
            src_ref=src, dst_ref=dst, send_sem=sems.at[0], recv_sem=sems.at[1],
            device_id=(target,), device_id_type=MESH,
        )

    loads = [
        pltpu.make_async_copy(tok, xt, load_sem.at[0]),
        pltpu.make_async_copy(og, gt, load_sem.at[1]),
        pltpu.make_async_copy(sw, sw_v, load_sem.at[2]),
        pltpu.make_async_copy(mw, mw_v, load_sem.at[3]),
        pltpu.make_async_copy(bias, bias_v, load_sem.at[4]),
        pltpu.make_async_copy(gate, gate_v, load_sem.at[5]),
    ]
    for load in loads:
        load.start()

    barrier = pltpu.get_barrier_semaphore()

    @pl.loop(1, GROUP)
    def _(j):
        pl.semaphore_signal(barrier, inc=1, device_id=(dev((top + j) % GROUP),), device_id_type=MESH)

    pl.semaphore_signal(barrier, inc=1, device_id=(mate,), device_id_type=MESH)
    for j in range(1, others):
        pl.semaphore_signal(
            barrier, inc=1, device_id=(mid_dev((mid + j) % others),), device_id_type=MESH
        )
    own = pl.ds(pl.multiple_of(top * sub, sub), sub)
    loads[0].wait()
    tok_v[...] = xt[...].T
    xin[own] = tok_v[own]
    loads[1].wait()
    og_v[...] = gt[...].T
    gin[own] = og_v[own]
    pl.semaphore_wait(barrier, GROUP + others - 1)

    def exchange(src, dst, number):
        def one(j):
            to = (top + j) % GROUP
            return remote(
                src.at[pl.ds(to * sub, sub)], dst.at[pl.ds(top * sub, sub)],
                a2a_sem.at[number, j], dev(to),
            )

        def start():
            @pl.loop(1, GROUP)
            def _(j):
                one(j).start()

        def received():
            @pl.loop(1, GROUP)
            def _(j):
                one(j).wait_recv()

        def sent():
            @pl.loop(1, GROUP)
            def _(j):
                one(j).wait_send()

        return start, received, sent

    tok_start, tok_received, tok_sent = exchange(tok_v, xin, 0)
    og_start, og_received, og_sent = exchange(og_v, gin, 1)
    net_start, net_received, net_sent = exchange(xs, net_o, 2)
    tg_start, tg_received, tg_sent = exchange(gs, tg_o, 3)
    tok_start()
    og_start()

    pad = wp.shape[1] - units
    loads[2].wait()
    loads[3].wait()
    turned = mw_v[...].T
    for h in range(2):
        wp[h, :units] = sw_v[h * units : (h + 1) * units]
        wp[h, units:] = jnp.zeros((pad, hidden_size), BF16)
        wt[h] = wp[h].T
        mt[h, :units] = turned[h * units : (h + 1) * units]
        mt[h, units:] = jnp.zeros((pad, hidden_size), BF16)
        mp[h] = mt[h].T
    loads[4].wait()
    loads[5].wait()
    rows_v[...] = jnp.zeros(rows_v.shape, F32)
    for h in range(2):
        rows_v[h : h + 1, :units] = jax.nn.sigmoid(gate_v[...].reshape(1, -1)[:, h * units : (h + 1) * units])
        rows_v[2 + h : 3 + h, :units] = bias_v[...].reshape(1, -1)[:, h * units : (h + 1) * units]
    sums[...] = jnp.zeros(sums.shape, F32)
    state[...] = jnp.zeros(state.shape, BF16)

    def spans(section):
        length = half >> section
        for k in range(2**section):
            for h in range(2):
                at = (2 * k + h) * length
                yield h, slice(k * length, (k + 1) * length), slice(at, at + length)

    chunk = 32
    tok_received()
    state[:, :units] = xin[...]
    for s in range(SECTIONS):
        for h, inner, outer in spans(s):
            sides[1, s, h, inner] = state[outer]
        pre[...] = dot(sides[1, s, 0], wp[0]) + dot(sides[1, s, 1], wp[1])

        @pl.loop(0, half // chunk)
        def _(i):
            at = pl.ds(pl.multiple_of(i * chunk, chunk), chunk)
            value = pre[at]
            centered = value - jnp.mean(value, -1, keepdims=True)
            scale = lax.rsqrt(jnp.mean(centered * centered, -1, keepdims=True) + 1e-05)
            value = centered * scale
            bell = jnp.exp2(value * value * (-0.5 * log2_e))
            phi_sum = distribution(value, bell)
            wides[0, s, at] = (value * phi_sum).astype(BF16)
            normed[s, at] = value
            slope[s, at] = phi_sum + value * bell * inv_sqrt_two_pi
            inv[s, at] = jnp.broadcast_to(scale, (chunk, LANES))

        outs = [
            (
                rows_v[h : h + 1] * sides[1, s, h].astype(F32)
                + 0.25 * (dot(wides[0, s], mp[h]) + rows_v[2 + h : 3 + h])
            ).astype(BF16)
            for h in range(2)
        ]
        for h, inner, outer in spans(s):
            if s < SECTIONS - 1:
                state[outer] = outs[h][inner]
            else:
                xs[outer] = outs[h][inner, :units]
    net_start()
    net_o[own] = xs[own]

    def gather_grads(side, wide, first):
        for h in range(2):
            term = dot(side[h].T[:units], wide[...])
            for c in range(hidden_size // LANES):
                at = slice((2 * c + h) * units, (2 * c + h + 1) * units)
                block = term[:, c * LANES : (c + 1) * LANES]
                flat[at] = block if first else flat[at] + block

    def mate_copies(s):
        return [
            remote(sides.at[1 - core, s], r_sides.at[s], mate_sem.at[0, s], mate),
            remote(wides.at[1 - core, s], r_wides.at[s], mate_sem.at[1, s], mate),
        ]

    vec_mate = remote(v0, rvm, vm_sem, mate)
    og_received()
    state[:, :units] = gin[...]
    for s in reversed(range(SECTIONS)):
        grads = [None, None]
        for h, inner, outer in spans(s):
            sides[0, s, h, inner] = (0.25 * state[outer].astype(F32)).astype(BF16)
        pre[...] = dot(sides[0, s, 0], mt[0]) + dot(sides[0, s, 1], mt[1])
        for h in range(2):
            value = 4.0 * sides[0, s, h].astype(F32)
            gated = value * sides[1, s, h].astype(F32)
            sums[h] += jnp.sum(value.reshape(-1, 8, value.shape[1]), 0)
            sums[2 + h] += jnp.sum(gated.reshape(-1, 8, value.shape[1]), 0)
        if s == 0:
            for r in range(4):
                v0[r : r + 1] = jnp.sum(sums[r], 0, keepdims=True)
            vec_mate.start()

        @pl.loop(0, half // chunk)
        def _(i):
            at = pl.ds(pl.multiple_of(i * chunk, chunk), chunk)
            value = normed[s, at]
            grad = pre[at] * slope[s, at]
            grad = (
                grad
                - jnp.mean(grad, -1, keepdims=True)
                - value * jnp.mean(grad * value, -1, keepdims=True)
            ) * inv[s, at][:, :1]
            wides[1, s, at] = grad.astype(BF16)

        for copy in mate_copies(s):
            copy.start()
        for h in range(2):
            back = dot(wides[1, s], wt[h])
            grads[h] = back
        for h, inner, outer in spans(s):
            value = (
                rows_v[h : h + 1] * (state[outer].astype(F32)) + grads[h][inner]
            ).astype(BF16)
            if s > 0:
                state[outer] = value
            else:
                gs[outer] = value[:, :units]
        if s == 0:
            tg_start()
            tg_o[own] = gs[own]
        gather_grads(sides.at[core, s], wides.at[core, s], s == SECTIONS - 1)
        if s < SECTIONS - 1:
            for copy in mate_copies(s + 1):
                copy.wait_recv()
            gather_grads(r_sides.at[s + 1], r_wides.at[s + 1], False)
    for copy in mate_copies(0):
        copy.wait_recv()
    gather_grads(r_sides.at[0], r_wides.at[0], False)
    flat_b[...] = flat[...].astype(BF16)

    def first_copies(j):
        to = (col + j) % SIDE
        target = dev(line * SIDE + to)
        return [
            remote(flat_b.at[pl.ds(to * quarter, quarter)], rv1.at[j - 1], rs1_sem.at[j], target),
            remote(v1, rvv1.at[j - 1], vv1_sem.at[j], target),
        ]

    def second_copies(j):
        to = (line + j) % SIDE
        target = dev(to * SIDE + col)
        return [
            remote(part_b.at[pl.ds(to * piece, piece)], rv2.at[j - 1], rs2_sem.at[j], target),
            remote(v2, rvv2.at[j - 1], vv2_sem.at[j], target),
        ]

    def other_copies(j):
        target = mid_dev((mid + j) % others)
        return [
            remote(last, rvx.at[j - 1], rsx_sem.at[j], target),
            remote(v3, rvvx.at[j - 1], vvx_sem.at[j], target),
        ]

    for j in range(1, SIDE):
        first_copies(j)[0].start()
    vec_mate.wait_recv()
    v1[...] = v0[...] + rvm[...]
    for j in range(1, SIDE):
        first_copies(j)[1].start()
    for j in range(1, SIDE):
        for copy in first_copies(j):
            copy.wait_recv()
    total = flat[pl.ds(pl.multiple_of(col * quarter, quarter), quarter)]
    for j in range(SIDE - 1):
        total = total + rv1[j].astype(F32)
    part[...] = total
    part_b[...] = total.astype(BF16)
    v2[...] = v1[...] + rvv1[0] + rvv1[1] + rvv1[2]
    for j in range(1, SIDE):
        for copy in second_copies(j):
            copy.start()
    for j in range(1, SIDE):
        for copy in second_copies(j):
            copy.wait_recv()
    total = part[pl.ds(pl.multiple_of(line * piece, piece), piece)]
    for j in range(SIDE - 1):
        total = total + rv2[j].astype(F32)
    vec = v2[...] + rvv2[0] + rvv2[1] + rvv2[2]
    if others > 1:
        last[...] = total.astype(BF16)
        v3[...] = vec
        for j in range(1, others):
            for copy in other_copies(j):
                copy.start()
        for j in range(1, others):
            for copy in other_copies(j):
                copy.wait_recv()
            total = total + rvx[j - 1].astype(F32)
            vec = vec + rvvx[j - 1]
    vec_o[...] = vec
    mine = pl.ds(pl.multiple_of(col * quarter + line * piece, piece), piece)
    res[core, mine] = total.astype(BF16)

    def line_copy(j):
        to = (line + j) % SIDE
        return remote(res.at[core, mine], res.at[core, mine], ag2_sem.at[j], dev(to * SIDE + col))

    whole = pl.ds(pl.multiple_of(col * quarter, quarter), quarter)

    def col_copy(j):
        to = (col + j) % SIDE
        return remote(res.at[core, whole], res.at[core, whole], ag1_sem.at[j], dev(line * SIDE + to))

    def mate_copy(j):
        at = (col + SIDE - j) % SIDE
        span = res.at[core, pl.ds(pl.multiple_of(at * quarter, quarter), quarter)]
        return remote(span, span, fwd_sem.at[j], mate)

    for j in range(1, SIDE):
        line_copy(j).start()
    for j in range(1, SIDE):
        line_copy(j).wait_recv()
    for j in range(1, SIDE):
        col_copy(j).start()
    mate_copy(0).start()
    for j in range(1, SIDE):
        col_copy(j).wait_recv()
        mate_copy(j).start()

    tok_sent()
    og_sent()
    net_sent()
    tg_sent()
    for s in range(SECTIONS):
        for copy in mate_copies(s):
            copy.wait_send()
    vec_mate.wait_send()
    for j in range(1, SIDE):
        for copy in first_copies(j) + second_copies(j) + [line_copy(j), col_copy(j)]:
            copy.wait_send()
    for j in range(1, others):
        for copy in other_copies(j):
            copy.wait_send()
    net_received()
    tg_received()
    for j in range(SIDE):
        mate_copy(j).wait()


def finish_kernel(scale, res, net, tg, vec, gate, net_o, tg_o, spread_o, merge_o, bias_o, gate_o):
    units = net.shape[1]
    tall, wide = spread_o.shape
    net_o[...] = net[...].T
    tg_o[...] = tg[...].T
    for c in range(wide // LANES):
        across = slice(c * LANES, (c + 1) * LANES)
        spread_o[:, across] = res[1, c * tall : (c + 1) * tall].astype(F32) * scale
        for k in range(tall // LANES):
            at = c * tall + k * LANES
            merge_o[across, k * LANES : (k + 1) * LANES] = (
                res[0, at : at + LANES].astype(F32) * scale
            ).T
    opened = jax.nn.sigmoid(gate[...])
    opened = opened * (1.0 - opened) * scale
    both = [
        jnp.concatenate([vec[r : r + 1, :units], vec[r + 1 : r + 2, :units]], 1) for r in (0, 2)
    ]
    bias_o[...] = both[0].reshape(-1) * (0.25 * scale)
    gate_o[...] = both[1].reshape(-1) * opened


def on_device(tokens, out_grad, spread_weight, merge_weight, switch_bias, gate_logit):
    n = lax.axis_size("seq")
    rows, units = tokens.shape
    switch, hidden_size = spread_weight.shape
    half = rows // 2
    wide_units = rounded_up(units)
    others = n // (2 * GROUP)
    more = max(others - 1, 1)
    flat_rows = switch * hidden_size // LANES
    quarter = flat_rows // SIDE
    piece = quarter // SIDE
    vec_shape = (4, wide_units)
    any_spec = pl.BlockSpec(memory_space=pltpu.HBM)
    vmem_spec = pl.BlockSpec(memory_space=pltpu.VMEM)
    dma = pltpu.SemaphoreType.DMA
    vmem = pltpu.VMEM
    net, tg, res, vec = pl.pallas_call(
        functools.partial(step_kernel, n),
        out_shape=(
            jax.ShapeDtypeStruct((rows, units), BF16),
            jax.ShapeDtypeStruct((rows, units), BF16),
            jax.ShapeDtypeStruct((2, flat_rows, LANES), BF16),
            jax.ShapeDtypeStruct(vec_shape, F32),
        ),
        in_specs=[any_spec] * 6,
        out_specs=(vmem_spec,) * 4,
        scratch_shapes=[
            vmem((switch, hidden_size), BF16),
            vmem((hidden_size, switch), BF16),
            vmem((switch,), F32),
            vmem((switch,), F32),
            vmem((units, rows), BF16),
            vmem((units, rows), BF16),
            vmem((rows, units), BF16),
            vmem((rows, units), BF16),
            vmem((rows, units), BF16),
            vmem((rows, units), BF16),
            vmem((rows, units), BF16),
            vmem((rows, units), BF16),
            vmem((rows, wide_units), BF16),
            vmem((2, wide_units, hidden_size), BF16),
            vmem((2, hidden_size, wide_units), BF16),
            vmem((2, hidden_size, wide_units), BF16),
            vmem((2, wide_units, hidden_size), BF16),
            vmem((8, wide_units), F32),
            vmem((2, SECTIONS, 2, half, wide_units), BF16),
            vmem((2, SECTIONS, half, hidden_size), BF16),
            vmem((SECTIONS, 2, half, wide_units), BF16),
            vmem((SECTIONS, half, hidden_size), BF16),
            vmem((half, hidden_size), F32),
            vmem((SECTIONS, half, hidden_size), F32),
            vmem((SECTIONS, half, hidden_size), F32),
            vmem((SECTIONS, half, LANES), F32),
            vmem((flat_rows, LANES), F32),
            vmem((flat_rows, LANES), BF16),
            vmem((quarter, LANES), F32),
            vmem((quarter, LANES), BF16),
            vmem((SIDE - 1, quarter, LANES), BF16),
            vmem((SIDE - 1, piece, LANES), BF16),
            vmem((more, piece, LANES), BF16),
            vmem((piece, LANES), BF16),
            vmem((4, 8, wide_units), F32),
            vmem(vec_shape, F32),
            vmem(vec_shape, F32),
            vmem(vec_shape, F32),
            vmem(vec_shape, F32),
            vmem(vec_shape, F32),
            vmem((SIDE - 1,) + vec_shape, F32),
            vmem((SIDE - 1,) + vec_shape, F32),
            vmem((more,) + vec_shape, F32),
            dma((6,)),
            dma((4, GROUP, 2)),
            dma((2, SECTIONS, 2)),
            dma((SIDE, 2)),
            dma((SIDE, 2)),
            dma((more + 1, 2)),
            dma((SIDE, 2)),
            dma((SIDE, 2)),
            dma((SIDE, 2)),
            dma((2,)),
            dma((SIDE, 2)),
            dma((SIDE, 2)),
            dma((more + 1, 2)),
        ],
        compiler_params=pltpu.CompilerParams(
            collective_id=0, has_side_effects=True, vmem_limit_bytes=48 * 2**20
        ),
        name="switch_step",
    )(tokens.T, out_grad.T, spread_weight, merge_weight, switch_bias, gate_logit)
    scale = 1.0 / math.sqrt(n * rows)
    net, tg, spread, merge, bias, gate = pl.pallas_call(
        functools.partial(finish_kernel, scale),
        out_shape=(
            jax.ShapeDtypeStruct((units, rows), BF16),
            jax.ShapeDtypeStruct((units, rows), BF16),
            jax.ShapeDtypeStruct((switch, hidden_size), F32),
            jax.ShapeDtypeStruct((hidden_size, switch), F32),
            jax.ShapeDtypeStruct((switch,), F32),
            jax.ShapeDtypeStruct((switch,), F32),
        ),
        in_specs=[vmem_spec] * 5,
        out_specs=(vmem_spec,) * 6,
        compiler_params=pltpu.CompilerParams(vmem_limit_bytes=32 * 2**20),
        name="finish",
    )(res, net, tg, vec, gate_logit)
    return net.T, tg.T, spread, merge, bias, gate


def solution(mesh):
    placed = (P("seq", None), P("seq", None), P(), P(), P(), P())
    return jax.shard_map(
        on_device,
        mesh=mesh,
        in_specs=placed,
        out_specs=placed,
        check_vma=False,
    )
```

```python
import functools
import math

import jax
import jax.numpy as jnp
from jax import lax
from jax.experimental import pallas as pl
from jax.experimental.pallas import tpu as pltpu
from jax.sharding import PartitionSpec as P

SECTIONS = 4
GROUP = 2**SECTIONS
SIDE = 4
LANES = 128
MESH = pl.DeviceIdType.MESH
F32 = jnp.float32
BF16 = jnp.bfloat16

log2_e = 1.4426950408889634
inv_sqrt_two_pi = 0.3989422804014327


def dot(a, b):
    return jnp.dot(a, b, preferred_element_type=F32)


def distribution(value, bell):
    base = 1.0 + (0.3275911 * 0.7071067811865476) * jnp.abs(value)
    guess = pl.reciprocal(base, approx=True)
    t = guess * (2.0 - base * guess)
    tail = 0.5 * 1.061405429
    for factor in (-1.453152027, 1.421413741, -0.284496736, 0.254829592):
        tail = tail * t + 0.5 * factor
    tail = tail * t * bell
    return jnp.where(value < 0.0, tail, 1.0 - tail)


def rounded_up(size):
    return -(-size // LANES) * LANES


def step_kernel(
    n,
    tok, og, sw, mw, bias, gate,
    net_o, tg_o, res, vec_o,
    sw_v, mw_v, bias_v, gate_v,
    xt, gt, tok_v, og_v, xin, gin, xs, gs,
    state, wp, wt, mp, mt, rows_v,
    sides, wides, r_sides, r_wides,
    pre, normed, slope, inv,
    flat, flat_b, part, part_b, rv1, rv2, rvx, last,
    sums, v0, v1, v2, v3, rvm, rvv1, rvv2, rvvx,
    load_sem, a2a_sem, mate_sem, rs1_sem, rs2_sem, rsx_sem, ag1_sem, ag2_sem, fwd_sem,
    vm_sem, vv1_sem, vv2_sem, vvx_sem,
):
    rows, units = xin.shape
    sub = rows // GROUP
    half = rows // 2
    hidden_size = sw_v.shape[1]
    stride = n // GROUP
    others = n // (2 * GROUP)
    blocks = rv1.shape[0]
    block_rows = flat.shape[0] // blocks
    quarter = block_rows // SIDE
    piece = quarter // SIDE

    me = lax.axis_index("seq")
    top = me // stride
    low = me % stride
    core = me % 2
    mid = low // 2
    mate = me + 1 - 2 * core
    col = top % SIDE
    line = top // SIDE

    def dev(which):
        return which * stride + low

    def mid_dev(which):
        return top * stride + which * 2 + core

    def remote(src, dst, sems, target):
        return pltpu.make_async_remote_copy(
            src_ref=src, dst_ref=dst, send_sem=sems.at[0], recv_sem=sems.at[1],
            device_id=(target,), device_id_type=MESH,
        )

    loads = [
        pltpu.make_async_copy(tok, xt, load_sem.at[0]),
        pltpu.make_async_copy(og, gt, load_sem.at[1]),
        pltpu.make_async_copy(sw, sw_v, load_sem.at[2]),
        pltpu.make_async_copy(mw, mw_v, load_sem.at[3]),
        pltpu.make_async_copy(bias, bias_v, load_sem.at[4]),
        pltpu.make_async_copy(gate, gate_v, load_sem.at[5]),
    ]
    for load in loads:
        load.start()

    barrier = pltpu.get_barrier_semaphore()

    @pl.loop(1, GROUP)
    def _(j):
        pl.semaphore_signal(barrier, inc=1, device_id=(dev((top + j) % GROUP),), device_id_type=MESH)

    pl.semaphore_signal(barrier, inc=1, device_id=(mate,), device_id_type=MESH)
    for j in range(1, others):
        pl.semaphore_signal(
            barrier, inc=1, device_id=(mid_dev((mid + j) % others),), device_id_type=MESH
        )
    own = pl.ds(pl.multiple_of(top * sub, sub), sub)
    loads[0].wait()
    tok_v[...] = xt[...].T
    xin[own] = tok_v[own]
    loads[1].wait()
    og_v[...] = gt[...].T
    gin[own] = og_v[own]
    pl.semaphore_wait(barrier, GROUP + others - 1)

    def exchange(src, dst, number):
        def one(j):
            to = (top + j) % GROUP
            return remote(
                src.at[pl.ds(to * sub, sub)], dst.at[pl.ds(top * sub, sub)],
                a2a_sem.at[number, j], dev(to),
            )

        def start():
            @pl.loop(1, GROUP)
            def _(j):
                one(j).start()

        def received():
            @pl.loop(1, GROUP)
            def _(j):
                one(j).wait_recv()

        def sent():
            @pl.loop(1, GROUP)
            def _(j):
                one(j).wait_send()

        return start, received, sent

    tok_start, tok_received, tok_sent = exchange(tok_v, xin, 0)
    og_start, og_received, og_sent = exchange(og_v, gin, 1)
    net_start, net_received, net_sent = exchange(xs, net_o, 2)
    tg_start, tg_received, tg_sent = exchange(gs, tg_o, 3)
    tok_start()

    pad = wp.shape[1] - units
    loads[2].wait()
    loads[3].wait()
    turned = mw_v[...].T
    for h in range(2):
        wp[h, :units] = sw_v[h * units : (h + 1) * units]
        wp[h, units:] = jnp.zeros((pad, hidden_size), BF16)
        wt[h] = wp[h].T
        mt[h, :units] = turned[h * units : (h + 1) * units]
        mt[h, units:] = jnp.zeros((pad, hidden_size), BF16)
        mp[h] = mt[h].T
    loads[4].wait()
    loads[5].wait()
    rows_v[...] = jnp.zeros(rows_v.shape, F32)
    for h in range(2):
        rows_v[h : h + 1, :units] = jax.nn.sigmoid(gate_v[...].reshape(1, -1)[:, h * units : (h + 1) * units])
        rows_v[2 + h : 3 + h, :units] = bias_v[...].reshape(1, -1)[:, h * units : (h + 1) * units]
    sums[...] = jnp.zeros(sums.shape, F32)
    state[...] = jnp.zeros(state.shape, BF16)

    def spans(section):
        length = half >> section
        for k in range(2**section):
            for h in range(2):
                at = (2 * k + h) * length
                yield h, slice(k * length, (k + 1) * length), slice(at, at + length)

    chunk = 16
    tok_received()
    og_start()
    state[:, :units] = xin[...]
    for s in range(SECTIONS):
        for h, inner, outer in spans(s):
            sides[1, s, h, inner] = state[outer]
        pre[...] = dot(sides[1, s, 0], wp[0]) + dot(sides[1, s, 1], wp[1])

        @pl.loop(0, half // chunk, unroll=4)
        def _(i):
            at = pl.ds(pl.multiple_of(i * chunk, chunk), chunk)
            value = pre[at]
            centered = value - jnp.mean(value, -1, keepdims=True)
            scale = lax.rsqrt(jnp.mean(centered * centered, -1, keepdims=True) + 1e-05)
            value = centered * scale
            bell = jnp.exp2(value * value * (-0.5 * log2_e))
            phi_sum = distribution(value, bell)
            wides[0, s, at] = (value * phi_sum).astype(BF16)
            normed[s, at] = value
            slope[s, at] = phi_sum + value * bell * inv_sqrt_two_pi
            inv[s, at] = jnp.broadcast_to(scale, (chunk, LANES))

        outs = [
            (
                rows_v[h : h + 1] * sides[1, s, h].astype(F32)
                + 0.25 * (dot(wides[0, s], mp[h]) + rows_v[2 + h : 3 + h])
            ).astype(BF16)
            for h in range(2)
        ]
        for h, inner, outer in spans(s):
            if s < SECTIONS - 1:
                state[outer] = outs[h][inner]
            else:
                xs[outer] = outs[h][inner, :units]
    net_start()
    net_o[own] = xs[own]

    def gather_grads(pairs, first=False, only=None):
        turned = [[side[h].T[:units] for h in range(2)] for side, _ in pairs]
        width = hidden_size // blocks
        for b in range(blocks):
            for h in range(2):
                term = sum(
                    dot(turned[k][h], wide[:, b * width : (b + 1) * width])
                    for k, (_, wide) in enumerate(pairs)
                )
                for c in range(width // LANES):
                    at = b * block_rows + (2 * c + h) * units
                    at = slice(at, at + units)
                    block = term[:, c * LANES : (c + 1) * LANES]
                    flat[at] = block if first else flat[at] + block
            if only is not None:
                only(b)

    def mate_copies(s):
        return [
            remote(sides.at[1 - core, s], r_sides.at[s], mate_sem.at[0, s], mate),
            remote(wides.at[1 - core, s], r_wides.at[s], mate_sem.at[1, s], mate),
        ]

    vec_mate = remote(v0, rvm, vm_sem, mate)
    og_received()
    state[:, :units] = gin[...]
    for s in reversed(range(SECTIONS)):
        grads = [None, None]
        for h, inner, outer in spans(s):
            sides[0, s, h, inner] = (0.25 * state[outer].astype(F32)).astype(BF16)
        pre[...] = dot(sides[0, s, 0], mt[0]) + dot(sides[0, s, 1], mt[1])
        for h in range(2):
            value = 4.0 * sides[0, s, h].astype(F32)
            gated = value * sides[1, s, h].astype(F32)
            sums[h] += jnp.sum(value.reshape(-1, 8, value.shape[1]), 0)
            sums[2 + h] += jnp.sum(gated.reshape(-1, 8, value.shape[1]), 0)
        if s == 0:
            for r in range(4):
                v0[r : r + 1] = jnp.sum(sums[r], 0, keepdims=True)
            vec_mate.start()

        @pl.loop(0, half // chunk, unroll=4)
        def _(i):
            at = pl.ds(pl.multiple_of(i * chunk, chunk), chunk)
            value = normed[s, at]
            grad = pre[at] * slope[s, at]
            grad = (
                grad
                - jnp.mean(grad, -1, keepdims=True)
                - value * jnp.mean(grad * value, -1, keepdims=True)
            ) * inv[s, at][:, :1]
            wides[1, s, at] = grad.astype(BF16)

        for copy in mate_copies(s):
            copy.start()
        for h in range(2):
            back = dot(wides[1, s], wt[h])
            grads[h] = back
        for h, inner, outer in spans(s):
            value = (
                rows_v[h : h + 1] * (state[outer].astype(F32)) + grads[h][inner]
            ).astype(BF16)
            if s > 0:
                state[outer] = value
            else:
                gs[outer] = value[:, :units]
        if s == 0:
            tg_start()
            tg_o[own] = gs[own]
        own_pair = (sides.at[core, s], wides.at[core, s])
        if s == SECTIONS - 1:
            gather_grads([own_pair], True)
        else:
            for copy in mate_copies(s + 1):
                copy.wait_recv()
            gather_grads([own_pair, (r_sides.at[s + 1], r_wides.at[s + 1])])

    def rows_at(b, first, size):
        return pl.ds(pl.multiple_of(b * block_rows + first, 16), size)

    def first_copy(b, j):
        to = (col + j) % SIDE
        return remote(
            flat_b.at[rows_at(b, to * quarter, quarter)], rv1.at[b, j - 1],
            rs1_sem.at[b, j], dev(line * SIDE + to),
        )

    def second_copy(b, j):
        to = (line + j) % SIDE
        return remote(
            part_b.at[b, pl.ds(pl.multiple_of(to * piece, piece), piece)], rv2.at[b, j - 1],
            rs2_sem.at[b, j], dev(to * SIDE + col),
        )

    def other_copy(b, j):
        return remote(
            last.at[b], rvx.at[b, j - 1], rsx_sem.at[b, j], mid_dev((mid + j) % others)
        )

    def line_copy(b, j):
        span = res.at[core, rows_at(b, col * quarter + line * piece, piece)]
        return remote(span, span, ag2_sem.at[b, j], dev((line + j) % SIDE * SIDE + col))

    def col_copy(b, j):
        span = res.at[core, rows_at(b, col * quarter, quarter)]
        return remote(span, span, ag1_sem.at[b, j], dev(line * SIDE + (col + j) % SIDE))

    def mate_copy(b, j):
        at = (col + SIDE - j) % SIDE
        span = res.at[core, rows_at(b, at * quarter, quarter)]
        return remote(span, span, fwd_sem.at[b, j], mate)

    def vec_first(j):
        return remote(v1, rvv1.at[j - 1], vv1_sem.at[j], dev(line * SIDE + (col + j) % SIDE))

    def vec_second(j):
        return remote(v2, rvv2.at[j - 1], vv2_sem.at[j], dev((line + j) % SIDE * SIDE + col))

    def vec_other(j):
        return remote(v3, rvvx.at[j - 1], vvx_sem.at[j], mid_dev((mid + j) % others))

    peers = range(1, SIDE)

    def send_block(b):
        at = slice(b * block_rows, (b + 1) * block_rows)
        flat_b[at] = flat[at].astype(BF16)
        for j in peers:
            first_copy(b, j).start()

    vec_mate.wait_recv()
    v1[...] = v0[...] + rvm[...]
    for j in peers:
        vec_first(j).start()
    for copy in mate_copies(0):
        copy.wait_recv()
    gather_grads([(r_sides.at[0], r_wides.at[0])], only=send_block)
    for b in range(blocks):
        for j in peers:
            first_copy(b, j).wait_recv()
        total = flat[rows_at(b, col * quarter, quarter)]
        for j in range(SIDE - 1):
            total = total + rv1[b, j].astype(F32)
        part[b] = total
        part_b[b] = total.astype(BF16)
        for j in peers:
            second_copy(b, j).start()
        if b == 0:
            for j in peers:
                vec_first(j).wait_recv()
            v2[...] = v1[...] + rvv1[0] + rvv1[1] + rvv1[2]
            for j in peers:
                vec_second(j).start()
    for b in range(blocks):
        for j in peers:
            second_copy(b, j).wait_recv()
        total = part[b, pl.ds(pl.multiple_of(line * piece, piece), piece)]
        for j in range(SIDE - 1):
            total = total + rv2[b, j].astype(F32)
        if others > 1:
            last[b] = total.astype(BF16)
            for j in range(1, others):
                other_copy(b, j).start()
            for j in range(1, others):
                other_copy(b, j).wait_recv()
                total = total + rvx[b, j - 1].astype(F32)
        res[core, rows_at(b, col * quarter + line * piece, piece)] = total.astype(BF16)
        for j in peers:
            line_copy(b, j).start()
    for j in peers:
        vec_second(j).wait_recv()
    vec = v2[...] + rvv2[0] + rvv2[1] + rvv2[2]
    if others > 1:
        v3[...] = vec
        for j in range(1, others):
            vec_other(j).start()
        for j in range(1, others):
            vec_other(j).wait_recv()
            vec = vec + rvvx[j - 1]
    vec_o[...] = vec
    for b in range(blocks):
        for j in peers:
            line_copy(b, j).wait_recv()
        for j in peers:
            col_copy(b, j).start()
        mate_copy(b, 0).start()
    for b in range(blocks):
        for j in peers:
            col_copy(b, j).wait_recv()
            mate_copy(b, j).start()

    tok_sent()
    og_sent()
    net_sent()
    tg_sent()
    for s in range(SECTIONS):
        for copy in mate_copies(s):
            copy.wait_send()
    vec_mate.wait_send()
    for j in peers:
        vec_first(j).wait_send()
        vec_second(j).wait_send()
        for b in range(blocks):
            for copy in (first_copy, second_copy, line_copy, col_copy):
                copy(b, j).wait_send()
    for j in range(1, others):
        vec_other(j).wait_send()
        for b in range(blocks):
            other_copy(b, j).wait_send()
    net_received()
    tg_received()
    for b in range(blocks):
        for j in range(SIDE):
            mate_copy(b, j).wait()


def finish_kernel(scale, res, net, tg, vec, gate, net_o, tg_o, spread_o, merge_o, bias_o, gate_o):
    units = net.shape[1]
    tall, wide = spread_o.shape
    net_o[...] = net[...].T
    tg_o[...] = tg[...].T
    for c in range(wide // LANES):
        across = slice(c * LANES, (c + 1) * LANES)
        spread_o[:, across] = res[1, c * tall : (c + 1) * tall].astype(F32) * scale
        for k in range(tall // LANES):
            at = c * tall + k * LANES
            merge_o[across, k * LANES : (k + 1) * LANES] = (
                res[0, at : at + LANES].astype(F32) * scale
            ).T
    opened = jax.nn.sigmoid(gate[...])
    opened = opened * (1.0 - opened) * scale
    both = [
        jnp.concatenate([vec[r : r + 1, :units], vec[r + 1 : r + 2, :units]], 1) for r in (0, 2)
    ]
    bias_o[...] = both[0].reshape(-1) * (0.25 * scale)
    gate_o[...] = both[1].reshape(-1) * opened


def on_device(tokens, out_grad, spread_weight, merge_weight, switch_bias, gate_logit):
    n = lax.axis_size("seq")
    rows, units = tokens.shape
    switch, hidden_size = spread_weight.shape
    half = rows // 2
    wide_units = rounded_up(units)
    others = n // (2 * GROUP)
    more = max(others - 1, 1)
    flat_rows = switch * hidden_size // LANES
    blocks = hidden_size // (2 * LANES)
    quarter = flat_rows // (blocks * SIDE)
    piece = quarter // SIDE
    vec_shape = (4, wide_units)
    any_spec = pl.BlockSpec(memory_space=pltpu.HBM)
    vmem_spec = pl.BlockSpec(memory_space=pltpu.VMEM)
    dma = pltpu.SemaphoreType.DMA
    vmem = pltpu.VMEM
    net, tg, res, vec = pl.pallas_call(
        functools.partial(step_kernel, n),
        out_shape=(
            jax.ShapeDtypeStruct((rows, units), BF16),
            jax.ShapeDtypeStruct((rows, units), BF16),
            jax.ShapeDtypeStruct((2, flat_rows, LANES), BF16),
            jax.ShapeDtypeStruct(vec_shape, F32),
        ),
        in_specs=[any_spec] * 6,
        out_specs=(vmem_spec,) * 4,
        scratch_shapes=[
            vmem((switch, hidden_size), BF16),
            vmem((hidden_size, switch), BF16),
            vmem((switch,), F32),
            vmem((switch,), F32),
            vmem((units, rows), BF16),
            vmem((units, rows), BF16),
            vmem((rows, units), BF16),
            vmem((rows, units), BF16),
            vmem((rows, units), BF16),
            vmem((rows, units), BF16),
            vmem((rows, units), BF16),
            vmem((rows, units), BF16),
            vmem((rows, wide_units), BF16),
            vmem((2, wide_units, hidden_size), BF16),
            vmem((2, hidden_size, wide_units), BF16),
            vmem((2, hidden_size, wide_units), BF16),
            vmem((2, wide_units, hidden_size), BF16),
            vmem((8, wide_units), F32),
            vmem((2, SECTIONS, 2, half, wide_units), BF16),
            vmem((2, SECTIONS, half, hidden_size), BF16),
            vmem((SECTIONS, 2, half, wide_units), BF16),
            vmem((SECTIONS, half, hidden_size), BF16),
            vmem((half, hidden_size), F32),
            vmem((SECTIONS, half, hidden_size), F32),
            vmem((SECTIONS, half, hidden_size), F32),
            vmem((SECTIONS, half, LANES), F32),
            vmem((flat_rows, LANES), F32),
            vmem((flat_rows, LANES), BF16),
            vmem((blocks, quarter, LANES), F32),
            vmem((blocks, quarter, LANES), BF16),
            vmem((blocks, SIDE - 1, quarter, LANES), BF16),
            vmem((blocks, SIDE - 1, piece, LANES), BF16),
            vmem((blocks, more, piece, LANES), BF16),
            vmem((blocks, piece, LANES), BF16),
            vmem((4, 8, wide_units), F32),
            vmem(vec_shape, F32),
            vmem(vec_shape, F32),
            vmem(vec_shape, F32),
            vmem(vec_shape, F32),
            vmem(vec_shape, F32),
            vmem((SIDE - 1,) + vec_shape, F32),
            vmem((SIDE - 1,) + vec_shape, F32),
            vmem((more,) + vec_shape, F32),
            dma((6,)),
            dma((4, GROUP, 2)),
            dma((2, SECTIONS, 2)),
            dma((blocks, SIDE, 2)),
            dma((blocks, SIDE, 2)),
            dma((blocks, more + 1, 2)),
            dma((blocks, SIDE, 2)),
            dma((blocks, SIDE, 2)),
            dma((blocks, SIDE, 2)),
            dma((2,)),
            dma((SIDE, 2)),
            dma((SIDE, 2)),
            dma((more + 1, 2)),
        ],
        compiler_params=pltpu.CompilerParams(
            collective_id=0, has_side_effects=True, vmem_limit_bytes=61 * 2**20
        ),
        name="switch_step",
    )(tokens.T, out_grad.T, spread_weight, merge_weight, switch_bias, gate_logit)
    scale = 1.0 / math.sqrt(n * rows)
    net, tg, spread, merge, bias, gate = pl.pallas_call(
        functools.partial(finish_kernel, scale),
        out_shape=(
            jax.ShapeDtypeStruct((units, rows), BF16),
            jax.ShapeDtypeStruct((units, rows), BF16),
            jax.ShapeDtypeStruct((switch, hidden_size), F32),
            jax.ShapeDtypeStruct((hidden_size, switch), F32),
            jax.ShapeDtypeStruct((switch,), F32),
            jax.ShapeDtypeStruct((switch,), F32),
        ),
        in_specs=[vmem_spec] * 5,
        out_specs=(vmem_spec,) * 6,
        compiler_params=pltpu.CompilerParams(vmem_limit_bytes=61 * 2**20),
        name="finish",
    )(res, net, tg, vec, gate_logit)
    return net.T, tg.T, spread, merge, bias, gate


def solution(mesh):
    placed = (P("seq", None), P("seq", None), P(), P(), P(), P())
    return jax.shard_map(
        on_device,
        mesh=mesh,
        in_specs=placed,
        out_specs=placed,
        check_vma=False,
    )
```

```python
import functools
import math

import jax
import jax.numpy as jnp
from jax import lax
from jax.experimental import pallas as pl
from jax.experimental.pallas import tpu as pltpu
from jax.sharding import PartitionSpec as P

SECTIONS = 4
GROUP = 2**SECTIONS
SIDE = 4
LANES = 128
MESH = pl.DeviceIdType.MESH
F32 = jnp.float32
BF16 = jnp.bfloat16

log2_e = 1.4426950408889634
inv_sqrt_two_pi = 0.3989422804014327


def dot(a, b):
    return jnp.dot(a, b, preferred_element_type=F32)


def distribution(value, bell):
    base = 1.0 + (0.3275911 * 0.7071067811865476) * jnp.abs(value)
    guess = pl.reciprocal(base, approx=True)
    t = guess * (2.0 - base * guess)
    tail = 0.5 * 1.061405429
    for factor in (-1.453152027, 1.421413741, -0.284496736, 0.254829592):
        tail = tail * t + 0.5 * factor
    tail = tail * t * bell
    return jnp.where(value < 0.0, tail, 1.0 - tail)


def weave(*tasks):
    steps = [
        ((k + 0.5) / len(task), number, step)
        for number, task in enumerate(tasks)
        for k, step in enumerate(task)
    ]
    for _, _, step in sorted(steps, key=lambda entry: entry[:2]):
        step()


def rounded_up(size):
    return -(-size // LANES) * LANES


def step_kernel(
    n,
    tok, og, sw, mw, bias, gate,
    net_o, tg_o, res, vec_o,
    sw_v, mw_v, bias_v, gate_v,
    xt, gt, tok_v, og_v, xin, gin, xs, gs,
    state, wp, wt, mp, mt, rows_v,
    sides, wides, r_sides, r_wides,
    pre, normed, slope, inv,
    flat, flat_b, part, part_b, rv1, rv2, rvx, last,
    sums, v0, v1, v2, v3, rvm, rvv1, rvv2, rvvx,
    load_sem, a2a_sem, mate_sem, rs1_sem, rs2_sem, rsx_sem, ag1_sem, ag2_sem, fwd_sem,
    vm_sem, vv1_sem, vv2_sem, vvx_sem,
):
    rows, units = xin.shape
    sub = rows // GROUP
    half = rows // 2
    hidden_size = sw_v.shape[1]
    stride = n // GROUP
    others = n // (2 * GROUP)
    blocks = rv1.shape[0]
    block_rows = flat.shape[0] // blocks
    quarter = block_rows // SIDE
    piece = quarter // SIDE

    me = lax.axis_index("seq")
    top = me // stride
    low = me % stride
    core = me % 2
    mid = low // 2
    mate = me + 1 - 2 * core
    col = top % SIDE
    line = top // SIDE

    def dev(which):
        return which * stride + low

    def mid_dev(which):
        return top * stride + which * 2 + core

    def remote(src, dst, sems, target):
        return pltpu.make_async_remote_copy(
            src_ref=src, dst_ref=dst, send_sem=sems.at[0], recv_sem=sems.at[1],
            device_id=(target,), device_id_type=MESH,
        )

    loads = [
        pltpu.make_async_copy(tok, xt, load_sem.at[0]),
        pltpu.make_async_copy(og, gt, load_sem.at[1]),
        pltpu.make_async_copy(sw, sw_v, load_sem.at[2]),
        pltpu.make_async_copy(mw, mw_v, load_sem.at[3]),
        pltpu.make_async_copy(bias, bias_v, load_sem.at[4]),
        pltpu.make_async_copy(gate, gate_v, load_sem.at[5]),
    ]
    for load in loads:
        load.start()

    barrier = pltpu.get_barrier_semaphore()

    @pl.loop(1, GROUP)
    def _(j):
        pl.semaphore_signal(barrier, inc=1, device_id=(dev((top + j) % GROUP),), device_id_type=MESH)

    pl.semaphore_signal(barrier, inc=1, device_id=(mate,), device_id_type=MESH)
    for j in range(1, others):
        pl.semaphore_signal(
            barrier, inc=1, device_id=(mid_dev((mid + j) % others),), device_id_type=MESH
        )
    own = pl.ds(pl.multiple_of(top * sub, sub), sub)
    loads[0].wait()
    tok_v[...] = xt[...].T
    xin[own] = tok_v[own]
    loads[1].wait()
    og_v[...] = gt[...].T
    gin[own] = og_v[own]
    pl.semaphore_wait(barrier, GROUP + others - 1)

    def exchange(src, dst, number):
        def one(j):
            to = (top + j) % GROUP
            return remote(
                src.at[pl.ds(to * sub, sub)], dst.at[pl.ds(top * sub, sub)],
                a2a_sem.at[number, j], dev(to),
            )

        def start():
            @pl.loop(1, GROUP)
            def _(j):
                one(j).start()

        def received():
            @pl.loop(1, GROUP)
            def _(j):
                one(j).wait_recv()

        def sent():
            @pl.loop(1, GROUP)
            def _(j):
                one(j).wait_send()

        return start, received, sent

    tok_start, tok_received, tok_sent = exchange(tok_v, xin, 0)
    og_start, og_received, og_sent = exchange(og_v, gin, 1)
    net_start, net_received, net_sent = exchange(xs, net_o, 2)
    tg_start, tg_received, tg_sent = exchange(gs, tg_o, 3)
    tok_start()

    pad = wp.shape[1] - units
    loads[2].wait()
    loads[3].wait()
    turned = mw_v[...].T
    for h in range(2):
        wp[h, :units] = sw_v[h * units : (h + 1) * units]
        wp[h, units:] = jnp.zeros((pad, hidden_size), BF16)
        wt[h] = wp[h].T
        mt[h, :units] = turned[h * units : (h + 1) * units]
        mt[h, units:] = jnp.zeros((pad, hidden_size), BF16)
        mp[h] = mt[h].T
    loads[4].wait()
    loads[5].wait()
    rows_v[...] = jnp.zeros(rows_v.shape, F32)
    for h in range(2):
        rows_v[h : h + 1, :units] = jax.nn.sigmoid(gate_v[...].reshape(1, -1)[:, h * units : (h + 1) * units])
        rows_v[2 + h : 3 + h, :units] = bias_v[...].reshape(1, -1)[:, h * units : (h + 1) * units]
    sums[...] = jnp.zeros(sums.shape, F32)
    state[...] = jnp.zeros(state.shape, BF16)

    chains = 2
    chain_rows = half // chains
    part_rows = sub // chains
    chunk = 16
    width = hidden_size // blocks

    def spans(section, chain):
        length = chain_rows >> section
        for k in range(2**section):
            for h in range(2):
                at = chain * rows // chains + (2 * k + h) * length
                inner = chain * chain_rows + k * length
                yield h, slice(inner, inner + length), slice(at, at + length)

    def rows_of(chain):
        return slice(chain * chain_rows, (chain + 1) * chain_rows)

    def split_chains(source):
        for chain in range(chains):
            for b in range(GROUP):
                at = (chain * GROUP + b) * part_rows
                start = b * sub + chain * part_rows
                state[at : at + part_rows, :units] = source[start : start + part_rows]

    def join_chains(target):
        for chain in range(chains):
            for b in range(GROUP):
                at = (chain * GROUP + b) * part_rows
                start = b * sub + chain * part_rows
                target[start : start + part_rows] = state[at : at + part_rows, :units]

    def products(left, weights, at):
        def one(b):
            cols = slice(b * width, (b + 1) * width)
            pre[at, cols] = dot(left[0, at], weights[0, :, cols]) + dot(
                left[1, at], weights[1, :, cols]
            )

        return [functools.partial(one, b) for b in range(blocks)]

    def lift(s, chain):
        def pairs():
            for h, inner, outer in spans(s, chain):
                sides[1, s, h, inner] = state[outer]

        return [pairs] + products(sides.at[1, s], wp, rows_of(chain))

    def act(s, chain):
        def one(i):
            at = slice(chain * chain_rows + i * chunk, chain * chain_rows + (i + 1) * chunk)
            value = pre[at]
            centered = value - jnp.mean(value, -1, keepdims=True)
            scale = lax.rsqrt(jnp.mean(centered * centered, -1, keepdims=True) + 1e-05)
            value = centered * scale
            bell = jnp.exp2(value * value * (-0.5 * log2_e))
            phi_sum = distribution(value, bell)
            wides[0, s, at] = (value * phi_sum).astype(BF16)
            normed[s, at] = value
            slope[s, at] = phi_sum + value * bell * inv_sqrt_two_pi
            inv[s, at] = jnp.broadcast_to(scale, (chunk, LANES))

        return [functools.partial(one, i) for i in range(chain_rows // chunk)]

    def drop(s, chain):
        at = rows_of(chain)

        def one(h):
            out = (
                rows_v[h : h + 1] * sides[1, s, h, at].astype(F32)
                + 0.25 * (dot(wides[0, s, at], mp[h]) + rows_v[2 + h : 3 + h])
            ).astype(BF16)
            for side, inner, outer in spans(s, chain):
                if side == h:
                    start = inner.start - at.start
                    state[outer] = out[start : start + inner.stop - inner.start]

        return [functools.partial(one, h) for h in range(2)]

    def lift_back(s, chain):
        at = rows_of(chain)

        def pairs():
            for h, inner, outer in spans(s, chain):
                sides[0, s, h, inner] = (0.25 * state[outer].astype(F32)).astype(BF16)

        def add_up():
            for h in range(2):
                value = 4.0 * sides[0, s, h, at].astype(F32)
                gated = value * sides[1, s, h, at].astype(F32)
                sums[h] += jnp.sum(value.reshape(-1, 8, value.shape[1]), 0)
                sums[2 + h] += jnp.sum(gated.reshape(-1, 8, value.shape[1]), 0)

        return [pairs] + products(sides.at[0, s], mt, at) + [add_up]

    def act_back(s, chain):
        def one(i):
            at = slice(chain * chain_rows + i * chunk, chain * chain_rows + (i + 1) * chunk)
            value = normed[s, at]
            grad = pre[at] * slope[s, at]
            grad = (
                grad
                - jnp.mean(grad, -1, keepdims=True)
                - value * jnp.mean(grad * value, -1, keepdims=True)
            ) * inv[s, at][:, :1]
            wides[1, s, at] = grad.astype(BF16)

        return [functools.partial(one, i) for i in range(chain_rows // chunk)]

    def drop_back(s, chain):
        at = rows_of(chain)

        def one(h):
            back = dot(wides[1, s, at], wt[h])
            for side, inner, outer in spans(s, chain):
                if side == h:
                    start = inner.start - at.start
                    state[outer] = (
                        rows_v[h : h + 1] * state[outer].astype(F32)
                        + back[start : start + inner.stop - inner.start]
                    ).astype(BF16)

        return [functools.partial(one, h) for h in range(2)]

    tok_received()
    og_start()
    split_chains(xin)
    order = [(s, chain) for s in range(SECTIONS) for chain in range(chains)]
    weave(lift(*order[0]))
    for k, phase in enumerate(order):
        beside = drop(*order[k - 1]) if k else []
        if k + 1 < len(order):
            beside += lift(*order[k + 1])
        weave(act(*phase), beside)
    weave(drop(*order[-1]))
    join_chains(xs)
    net_start()
    net_o[own] = xs[own]

    def gather_grads(pairs, first=False, only=None):
        turned = {}

        def turn(k, h):
            turned[k, h] = pairs[k][0][h].T[:units]

        def one(b, h):
            term = sum(
                dot(turned[k, h], wide[:, b * width : (b + 1) * width])
                for k, (_, wide) in enumerate(pairs)
            )
            for c in range(width // LANES):
                at = b * block_rows + (2 * c + h) * units
                at = slice(at, at + units)
                block = term[:, c * LANES : (c + 1) * LANES]
                flat[at] = block if first else flat[at] + block
            if only is not None and h == 1:
                only(b)

        steps = [functools.partial(turn, k, h) for k in range(len(pairs)) for h in range(2)]
        return steps + [functools.partial(one, b, h) for b in range(blocks) for h in range(2)]

    def mate_copies(s):
        return [
            remote(sides.at[1 - core, s], r_sides.at[s], mate_sem.at[0, s], mate),
            remote(wides.at[1 - core, s], r_wides.at[s], mate_sem.at[1, s], mate),
        ]

    vec_mate = remote(v0, rvm, vm_sem, mate)
    og_received()
    split_chains(gin)

    def own_pair(s):
        return sides.at[core, s], wides.at[core, s]

    def mate_pair(s):
        for copy in mate_copies(s):
            copy.wait_recv()
        return r_sides.at[s], r_wides.at[s]

    order = [(s, chain) for s in reversed(range(SECTIONS)) for chain in range(chains)]
    weave(lift_back(*order[0]))
    for k, (s, chain) in enumerate(order):
        beside = drop_back(*order[k - 1]) if k else []
        if chain == 0 and s < SECTIONS - 1:
            for copy in mate_copies(s + 1):
                copy.start()
            pairs = [own_pair(s + 1)]
            if s < SECTIONS - 2:
                pairs.append(mate_pair(s + 2))
            beside += gather_grads(pairs, s == SECTIONS - 2)
        if k + 1 < len(order):
            beside += lift_back(*order[k + 1])
        else:
            for r in range(4):
                v0[r : r + 1] = jnp.sum(sums[r], 0, keepdims=True)
            vec_mate.start()
        weave(act_back(s, chain), beside)
    for copy in mate_copies(0):
        copy.start()
    weave(drop_back(*order[-1]))
    join_chains(gs)
    tg_start()
    tg_o[own] = gs[own]
    weave(gather_grads([own_pair(0), mate_pair(1)]))

    def rows_at(b, first, size):
        return pl.ds(pl.multiple_of(b * block_rows + first, 16), size)

    def first_copy(b, j):
        to = (col + j) % SIDE
        return remote(
            flat_b.at[rows_at(b, to * quarter, quarter)], rv1.at[b, j - 1],
            rs1_sem.at[b, j], dev(line * SIDE + to),
        )

    def second_copy(b, j):
        to = (line + j) % SIDE
        return remote(
            part_b.at[b, pl.ds(pl.multiple_of(to * piece, piece), piece)], rv2.at[b, j - 1],
            rs2_sem.at[b, j], dev(to * SIDE + col),
        )

    def other_copy(b, j):
        return remote(
            last.at[b], rvx.at[b, j - 1], rsx_sem.at[b, j], mid_dev((mid + j) % others)
        )

    def line_copy(b, j):
        span = res.at[core, rows_at(b, col * quarter + line * piece, piece)]
        return remote(span, span, ag2_sem.at[b, j], dev((line + j) % SIDE * SIDE + col))

    def col_copy(b, j):
        span = res.at[core, rows_at(b, col * quarter, quarter)]
        return remote(span, span, ag1_sem.at[b, j], dev(line * SIDE + (col + j) % SIDE))

    def mate_copy(b, j):
        at = (col + SIDE - j) % SIDE
        span = res.at[core, rows_at(b, at * quarter, quarter)]
        return remote(span, span, fwd_sem.at[b, j], mate)

    def vec_first(j):
        return remote(v1, rvv1.at[j - 1], vv1_sem.at[j], dev(line * SIDE + (col + j) % SIDE))

    def vec_second(j):
        return remote(v2, rvv2.at[j - 1], vv2_sem.at[j], dev((line + j) % SIDE * SIDE + col))

    def vec_other(j):
        return remote(v3, rvvx.at[j - 1], vvx_sem.at[j], mid_dev((mid + j) % others))

    peers = range(1, SIDE)

    def send_block(b):
        at = slice(b * block_rows, (b + 1) * block_rows)
        flat_b[at] = flat[at].astype(BF16)
        for j in peers:
            first_copy(b, j).start()

    vec_mate.wait_recv()
    v1[...] = v0[...] + rvm[...]
    for j in peers:
        vec_first(j).start()
    weave(gather_grads([mate_pair(0)], only=send_block))
    for b in range(blocks):
        for j in peers:
            first_copy(b, j).wait_recv()
        total = flat[rows_at(b, col * quarter, quarter)]
        for j in range(SIDE - 1):
            total = total + rv1[b, j].astype(F32)
        part[b] = total
        part_b[b] = total.astype(BF16)
        for j in peers:
            second_copy(b, j).start()
        if b == 0:
            for j in peers:
                vec_first(j).wait_recv()
            v2[...] = v1[...] + rvv1[0] + rvv1[1] + rvv1[2]
            for j in peers:
                vec_second(j).start()
    for b in range(blocks):
        for j in peers:
            second_copy(b, j).wait_recv()
        total = part[b, pl.ds(pl.multiple_of(line * piece, piece), piece)]
        for j in range(SIDE - 1):
            total = total + rv2[b, j].astype(F32)
        if others > 1:
            last[b] = total.astype(BF16)
            for j in range(1, others):
                other_copy(b, j).start()
            for j in range(1, others):
                other_copy(b, j).wait_recv()
                total = total + rvx[b, j - 1].astype(F32)
        res[core, rows_at(b, col * quarter + line * piece, piece)] = total.astype(BF16)
        for j in peers:
            line_copy(b, j).start()
    for j in peers:
        vec_second(j).wait_recv()
    vec = v2[...] + rvv2[0] + rvv2[1] + rvv2[2]
    if others > 1:
        v3[...] = vec
        for j in range(1, others):
            vec_other(j).start()
        for j in range(1, others):
            vec_other(j).wait_recv()
            vec = vec + rvvx[j - 1]
    vec_o[...] = vec
    for b in range(blocks):
        for j in peers:
            line_copy(b, j).wait_recv()
        for j in peers:
            col_copy(b, j).start()
        mate_copy(b, 0).start()
    for b in range(blocks):
        for j in peers:
            col_copy(b, j).wait_recv()
            mate_copy(b, j).start()

    tok_sent()
    og_sent()
    net_sent()
    tg_sent()
    for s in range(SECTIONS):
        for copy in mate_copies(s):
            copy.wait_send()
    vec_mate.wait_send()
    for j in peers:
        vec_first(j).wait_send()
        vec_second(j).wait_send()
        for b in range(blocks):
            for copy in (first_copy, second_copy, line_copy, col_copy):
                copy(b, j).wait_send()
    for j in range(1, others):
        vec_other(j).wait_send()
        for b in range(blocks):
            other_copy(b, j).wait_send()
    net_received()
    tg_received()
    for b in range(blocks):
        for j in range(SIDE):
            mate_copy(b, j).wait()


def finish_kernel(scale, res, net, tg, vec, gate, net_o, tg_o, spread_o, merge_o, bias_o, gate_o):
    units = net.shape[1]
    tall, wide = spread_o.shape
    net_o[...] = net[...].T
    tg_o[...] = tg[...].T
    for c in range(wide // LANES):
        across = slice(c * LANES, (c + 1) * LANES)
        spread_o[:, across] = res[1, c * tall : (c + 1) * tall].astype(F32) * scale
        for k in range(tall // LANES):
            at = c * tall + k * LANES
            merge_o[across, k * LANES : (k + 1) * LANES] = (
                res[0, at : at + LANES].astype(F32) * scale
            ).T
    opened = jax.nn.sigmoid(gate[...])
    opened = opened * (1.0 - opened) * scale
    both = [
        jnp.concatenate([vec[r : r + 1, :units], vec[r + 1 : r + 2, :units]], 1) for r in (0, 2)
    ]
    bias_o[...] = both[0].reshape(-1) * (0.25 * scale)
    gate_o[...] = both[1].reshape(-1) * opened


def on_device(tokens, out_grad, spread_weight, merge_weight, switch_bias, gate_logit):
    n = lax.axis_size("seq")
    rows, units = tokens.shape
    switch, hidden_size = spread_weight.shape
    half = rows // 2
    wide_units = rounded_up(units)
    others = n // (2 * GROUP)
    more = max(others - 1, 1)
    flat_rows = switch * hidden_size // LANES
    blocks = hidden_size // (2 * LANES)
    quarter = flat_rows // (blocks * SIDE)
    piece = quarter // SIDE
    vec_shape = (4, wide_units)
    any_spec = pl.BlockSpec(memory_space=pltpu.HBM)
    vmem_spec = pl.BlockSpec(memory_space=pltpu.VMEM)
    dma = pltpu.SemaphoreType.DMA
    vmem = pltpu.VMEM
    net, tg, res, vec = pl.pallas_call(
        functools.partial(step_kernel, n),
        out_shape=(
            jax.ShapeDtypeStruct((rows, units), BF16),
            jax.ShapeDtypeStruct((rows, units), BF16),
            jax.ShapeDtypeStruct((2, flat_rows, LANES), BF16),
            jax.ShapeDtypeStruct(vec_shape, F32),
        ),
        in_specs=[any_spec] * 6,
        out_specs=(vmem_spec,) * 4,
        scratch_shapes=[
            vmem((switch, hidden_size), BF16),
            vmem((hidden_size, switch), BF16),
            vmem((switch,), F32),
            vmem((switch,), F32),
            vmem((units, rows), BF16),
            vmem((units, rows), BF16),
            vmem((rows, units), BF16),
            vmem((rows, units), BF16),
            vmem((rows, units), BF16),
            vmem((rows, units), BF16),
            vmem((rows, units), BF16),
            vmem((rows, units), BF16),
            vmem((rows, wide_units), BF16),
            vmem((2, wide_units, hidden_size), BF16),
            vmem((2, hidden_size, wide_units), BF16),
            vmem((2, hidden_size, wide_units), BF16),
            vmem((2, wide_units, hidden_size), BF16),
            vmem((8, wide_units), F32),
            vmem((2, SECTIONS, 2, half, wide_units), BF16),
            vmem((2, SECTIONS, half, hidden_size), BF16),
            vmem((SECTIONS, 2, half, wide_units), BF16),
            vmem((SECTIONS, half, hidden_size), BF16),
            vmem((half, hidden_size), F32),
            vmem((SECTIONS, half, hidden_size), F32),
            vmem((SECTIONS, half, hidden_size), F32),
            vmem((SECTIONS, half, LANES), F32),
            vmem((flat_rows, LANES), F32),
            vmem((flat_rows, LANES), BF16),
            vmem((blocks, quarter, LANES), F32),
            vmem((blocks, quarter, LANES), BF16),
            vmem((blocks, SIDE - 1, quarter, LANES), BF16),
            vmem((blocks, SIDE - 1, piece, LANES), BF16),
            vmem((blocks, more, piece, LANES), BF16),
            vmem((blocks, piece, LANES), BF16),
            vmem((4, 8, wide_units), F32),
            vmem(vec_shape, F32),
            vmem(vec_shape, F32),
            vmem(vec_shape, F32),
            vmem(vec_shape, F32),
            vmem(vec_shape, F32),
            vmem((SIDE - 1,) + vec_shape, F32),
            vmem((SIDE - 1,) + vec_shape, F32),
            vmem((more,) + vec_shape, F32),
            dma((6,)),
            dma((4, GROUP, 2)),
            dma((2, SECTIONS, 2)),
            dma((blocks, SIDE, 2)),
            dma((blocks, SIDE, 2)),
            dma((blocks, more + 1, 2)),
            dma((blocks, SIDE, 2)),
            dma((blocks, SIDE, 2)),
            dma((blocks, SIDE, 2)),
            dma((2,)),
            dma((SIDE, 2)),
            dma((SIDE, 2)),
            dma((more + 1, 2)),
        ],
        compiler_params=pltpu.CompilerParams(
            collective_id=0, has_side_effects=True, vmem_limit_bytes=61 * 2**20
        ),
        name="switch_step",
    )(tokens.T, out_grad.T, spread_weight, merge_weight, switch_bias, gate_logit)
    scale = 1.0 / math.sqrt(n * rows)
    net, tg, spread, merge, bias, gate = pl.pallas_call(
        functools.partial(finish_kernel, scale),
        out_shape=(
            jax.ShapeDtypeStruct((units, rows), BF16),
            jax.ShapeDtypeStruct((units, rows), BF16),
            jax.ShapeDtypeStruct((switch, hidden_size), F32),
            jax.ShapeDtypeStruct((hidden_size, switch), F32),
            jax.ShapeDtypeStruct((switch,), F32),
            jax.ShapeDtypeStruct((switch,), F32),
        ),
        in_specs=[vmem_spec] * 5,
        out_specs=(vmem_spec,) * 6,
        compiler_params=pltpu.CompilerParams(vmem_limit_bytes=61 * 2**20),
        name="finish",
    )(res, net, tg, vec, gate_logit)
    return net.T, tg.T, spread, merge, bias, gate


def solution(mesh):
    placed = (P("seq", None), P("seq", None), P(), P(), P(), P())
    return jax.shard_map(
        on_device,
        mesh=mesh,
        in_specs=placed,
        out_specs=placed,
        check_vma=False,
    )
```

```python
import functools
import math

import jax
import jax.numpy as jnp
from jax import lax
from jax.experimental import pallas as pl
from jax.experimental.pallas import tpu as pltpu
from jax.sharding import PartitionSpec as P

SECTIONS = 4
GROUP = 2**SECTIONS
SIDE = 4
LANES = 128
MESH = pl.DeviceIdType.MESH
F32 = jnp.float32
BF16 = jnp.bfloat16

log2_e = 1.4426950408889634
inv_sqrt_two_pi = 0.3989422804014327


def dot(a, b):
    return jnp.dot(a, b, preferred_element_type=F32)


def distribution(value, bell):
    base = 1.0 + (0.3275911 * 0.7071067811865476) * jnp.abs(value)
    guess = pl.reciprocal(base, approx=True)
    t = guess * (2.0 - base * guess)
    tail = 0.5 * 1.061405429
    for factor in (-1.453152027, 1.421413741, -0.284496736, 0.254829592):
        tail = tail * t + 0.5 * factor
    tail = tail * t * bell
    return jnp.where(value < 0.0, tail, 1.0 - tail)


def weave(*tasks):
    steps = [
        ((k + 0.5) / len(task), number, step)
        for number, task in enumerate(tasks)
        for k, step in enumerate(task)
    ]
    for _, _, step in sorted(steps, key=lambda entry: entry[:2]):
        step()


def rounded_up(size):
    return -(-size // LANES) * LANES


def step_kernel(
    n,
    tok, og, sw, mw, bias, gate,
    net_o, tg_o, res, vec_o,
    sw_v, mw_v, bias_v, gate_v,
    xt, gt, tok_v, og_v, xin, gin, xs, gs,
    state, wp, wt, mp, mt, rows_v,
    sides, wides, r_sides, r_wides,
    pre, normed, slope, inv,
    flat, flat_b, part, part_b, rv1, rv2, rvx, last,
    sums, v0, v1, v2, v3, rvm, rvv1, rvv2, rvvx,
    load_sem, a2a_sem, mate_sem, rs1_sem, rs2_sem, rsx_sem, ag1_sem, ag2_sem, fwd_sem,
    vm_sem, vv1_sem, vv2_sem, vvx_sem,
):
    rows, units = xin.shape
    sub = rows // GROUP
    half = rows // 2
    hidden_size = sw_v.shape[1]
    stride = n // GROUP
    others = n // (2 * GROUP)
    blocks = rv1.shape[0]
    block_rows = flat.shape[0] // blocks
    quarter = block_rows // SIDE
    piece = quarter // SIDE

    me = lax.axis_index("seq")
    top = me // stride
    low = me % stride
    core = me % 2
    mid = low // 2
    mate = me + 1 - 2 * core
    col = top % SIDE
    line = top // SIDE

    def dev(which):
        return which * stride + low

    def mid_dev(which):
        return top * stride + which * 2 + core

    def remote(src, dst, sems, target):
        return pltpu.make_async_remote_copy(
            src_ref=src, dst_ref=dst, send_sem=sems.at[0], recv_sem=sems.at[1],
            device_id=(target,), device_id_type=MESH,
        )

    loads = [
        pltpu.make_async_copy(tok, xt, load_sem.at[0]),
        pltpu.make_async_copy(og, gt, load_sem.at[1]),
        pltpu.make_async_copy(sw, sw_v, load_sem.at[2]),
        pltpu.make_async_copy(mw, mw_v, load_sem.at[3]),
        pltpu.make_async_copy(bias, bias_v, load_sem.at[4]),
        pltpu.make_async_copy(gate, gate_v, load_sem.at[5]),
    ]
    for load in loads:
        load.start()

    barrier = pltpu.get_barrier_semaphore()

    @pl.loop(1, GROUP)
    def _(j):
        pl.semaphore_signal(barrier, inc=1, device_id=(dev((top + j) % GROUP),), device_id_type=MESH)

    pl.semaphore_signal(barrier, inc=1, device_id=(mate,), device_id_type=MESH)
    for j in range(1, others):
        pl.semaphore_signal(
            barrier, inc=1, device_id=(mid_dev((mid + j) % others),), device_id_type=MESH
        )
    own = pl.ds(pl.multiple_of(top * sub, sub), sub)
    loads[0].wait()
    tok_v[...] = xt[...].T
    xin[own] = tok_v[own]
    pl.semaphore_wait(barrier, GROUP + others - 1)

    def exchange(src, dst, number):
        def one(j):
            to = (top + j) % GROUP
            return remote(
                src.at[pl.ds(to * sub, sub)], dst.at[pl.ds(top * sub, sub)],
                a2a_sem.at[number, j], dev(to),
            )

        def start():
            @pl.loop(1, GROUP)
            def _(j):
                one(j).start()

        def received():
            @pl.loop(1, GROUP)
            def _(j):
                one(j).wait_recv()

        def sent():
            @pl.loop(1, GROUP)
            def _(j):
                one(j).wait_send()

        return start, received, sent

    tok_start, tok_received, tok_sent = exchange(tok_v, xin, 0)
    og_start, og_received, og_sent = exchange(og_v, gin, 1)
    net_start, net_received, net_sent = exchange(xs, net_o, 2)
    tg_start, tg_received, tg_sent = exchange(gs, tg_o, 3)
    tok_start()
    loads[1].wait()
    og_v[...] = gt[...].T
    gin[own] = og_v[own]

    pad = wp.shape[1] - units
    loads[2].wait()
    loads[3].wait()
    turned = mw_v[...].T
    for h in range(2):
        wp[h, :units] = sw_v[h * units : (h + 1) * units]
        wp[h, units:] = jnp.zeros((pad, hidden_size), BF16)
        wt[h] = wp[h].T
        mt[h, :units] = turned[h * units : (h + 1) * units]
        mt[h, units:] = jnp.zeros((pad, hidden_size), BF16)
        mp[h] = mt[h].T
    loads[4].wait()
    loads[5].wait()
    rows_v[...] = jnp.zeros(rows_v.shape, F32)
    for h in range(2):
        rows_v[h : h + 1, :units] = jax.nn.sigmoid(gate_v[...].reshape(1, -1)[:, h * units : (h + 1) * units])
        rows_v[2 + h : 3 + h, :units] = bias_v[...].reshape(1, -1)[:, h * units : (h + 1) * units]
    sums[...] = jnp.zeros(sums.shape, F32)
    state[...] = jnp.zeros(state.shape, BF16)

    chains = 2
    chain_rows = half // chains
    part_rows = sub // chains
    chunk = 16
    width = hidden_size // blocks

    def spans(section, chain):
        length = chain_rows >> section
        for k in range(2**section):
            for h in range(2):
                at = chain * rows // chains + (2 * k + h) * length
                inner = chain * chain_rows + k * length
                yield h, slice(inner, inner + length), slice(at, at + length)

    def rows_of(chain):
        return slice(chain * chain_rows, (chain + 1) * chain_rows)

    def split_chains(source):
        for chain in range(chains):
            for b in range(GROUP):
                at = (chain * GROUP + b) * part_rows
                start = b * sub + chain * part_rows
                state[at : at + part_rows, :units] = source[start : start + part_rows]

    def join_chains(target):
        for chain in range(chains):
            for b in range(GROUP):
                at = (chain * GROUP + b) * part_rows
                start = b * sub + chain * part_rows
                target[start : start + part_rows] = state[at : at + part_rows, :units]

    def products(left, weights, at):
        def one(b):
            cols = slice(b * width, (b + 1) * width)
            pre[at, cols] = dot(left[0, at], weights[0, :, cols]) + dot(
                left[1, at], weights[1, :, cols]
            )

        return [functools.partial(one, b) for b in range(blocks)]

    def lift(s, chain):
        def pairs():
            for h, inner, outer in spans(s, chain):
                sides[1, s, h, inner] = state[outer]

        return [pairs] + products(sides.at[1, s], wp, rows_of(chain))

    def act(s, chain):
        def one(i):
            at = slice(chain * chain_rows + i * chunk, chain * chain_rows + (i + 1) * chunk)
            value = pre[at]
            centered = value - jnp.mean(value, -1, keepdims=True)
            scale = lax.rsqrt(jnp.mean(centered * centered, -1, keepdims=True) + 1e-05)
            value = centered * scale
            bell = jnp.exp2(value * value * (-0.5 * log2_e))
            phi_sum = distribution(value, bell)
            wides[0, s, at] = (value * phi_sum).astype(BF16)
            normed[s, at] = value
            slope[s, at] = phi_sum + value * bell * inv_sqrt_two_pi
            inv[s, at] = jnp.broadcast_to(scale, (chunk, LANES))

        return [functools.partial(one, i) for i in range(chain_rows // chunk)]

    def drop(s, chain):
        at = rows_of(chain)

        def one(h):
            out = (
                rows_v[h : h + 1] * sides[1, s, h, at].astype(F32)
                + 0.25 * (dot(wides[0, s, at], mp[h]) + rows_v[2 + h : 3 + h])
            ).astype(BF16)
            for side, inner, outer in spans(s, chain):
                if side == h:
                    start = inner.start - at.start
                    state[outer] = out[start : start + inner.stop - inner.start]

        return [functools.partial(one, h) for h in range(2)]

    def lift_back(s, chain):
        at = rows_of(chain)

        def pairs():
            for h, inner, outer in spans(s, chain):
                sides[0, s, h, inner] = (0.25 * state[outer].astype(F32)).astype(BF16)

        def add_up():
            for h in range(2):
                value = 4.0 * sides[0, s, h, at].astype(F32)
                gated = value * sides[1, s, h, at].astype(F32)
                sums[h] += jnp.sum(value.reshape(-1, 8, value.shape[1]), 0)
                sums[2 + h] += jnp.sum(gated.reshape(-1, 8, value.shape[1]), 0)

        return [pairs] + products(sides.at[0, s], mt, at) + [add_up]

    def act_back(s, chain):
        def one(i):
            at = slice(chain * chain_rows + i * chunk, chain * chain_rows + (i + 1) * chunk)
            value = normed[s, at]
            grad = pre[at] * slope[s, at]
            grad = (
                grad
                - jnp.mean(grad, -1, keepdims=True)
                - value * jnp.mean(grad * value, -1, keepdims=True)
            ) * inv[s, at][:, :1]
            wides[1, s, at] = grad.astype(BF16)

        return [functools.partial(one, i) for i in range(chain_rows // chunk)]

    def drop_back(s, chain):
        at = rows_of(chain)

        def one(h):
            back = dot(wides[1, s, at], wt[h])
            for side, inner, outer in spans(s, chain):
                if side == h:
                    start = inner.start - at.start
                    state[outer] = (
                        rows_v[h : h + 1] * state[outer].astype(F32)
                        + back[start : start + inner.stop - inner.start]
                    ).astype(BF16)

        return [functools.partial(one, h) for h in range(2)]

    tok_received()
    og_start()
    split_chains(xin)
    order = [(s, chain) for s in range(SECTIONS) for chain in range(chains)]
    weave(lift(*order[0]))
    for k, phase in enumerate(order):
        beside = drop(*order[k - 1]) if k else []
        if k + 1 < len(order):
            beside += lift(*order[k + 1])
        weave(act(*phase), beside)
    weave(drop(*order[-1]))
    join_chains(xs)
    net_start()
    net_o[own] = xs[own]

    def gather_grads(pairs, first=False, only=None):
        turned = {}

        def turn(k, h):
            turned[k, h] = pairs[k][0][h].T[:units]

        def one(b, h):
            term = sum(
                dot(turned[k, h], wide[:, b * width : (b + 1) * width])
                for k, (_, wide) in enumerate(pairs)
            )
            for c in range(width // LANES):
                at = b * block_rows + (2 * c + h) * units
                at = slice(at, at + units)
                block = term[:, c * LANES : (c + 1) * LANES]
                flat[at] = block if first else flat[at] + block
            if only is not None and h == 1:
                only(b)

        steps = [functools.partial(turn, k, h) for k in range(len(pairs)) for h in range(2)]
        return steps + [functools.partial(one, b, h) for b in range(blocks) for h in range(2)]

    def mate_copies(s):
        return [
            remote(sides.at[1 - core, s], r_sides.at[s], mate_sem.at[0, s], mate),
            remote(wides.at[1 - core, s], r_wides.at[s], mate_sem.at[1, s], mate),
        ]

    vec_mate = remote(v0, rvm, vm_sem, mate)
    og_received()
    split_chains(gin)

    def own_pair(s):
        return sides.at[core, s], wides.at[core, s]

    def mate_pair(s):
        for copy in mate_copies(s):
            copy.wait_recv()
        return r_sides.at[s], r_wides.at[s]

    def send_wide(s, sender):
        @pl.when(core == sender)
        def _():
            mate_copies(s)[1].start()

    order = [(s, chain) for s in reversed(range(SECTIONS)) for chain in range(chains)]
    weave(lift_back(*order[0]))
    for k, (s, chain) in enumerate(order):
        beside = drop_back(*order[k - 1]) if k else []
        if chain == 0 and s < SECTIONS - 1:
            send_wide(s + 1, 0)
            pairs = [own_pair(s + 1)]
            if s < SECTIONS - 2:
                pairs.append(mate_pair(s + 2))
            beside += gather_grads(pairs, s == SECTIONS - 2)
        if chain == 1:
            mate_copies(s)[0].start()
            send_wide(s, 1)
        if (s, chain) == (0, 1):
            beside += gather_grads([mate_pair(1)])
        if k + 1 < len(order):
            beside += lift_back(*order[k + 1])
        else:
            for r in range(4):
                v0[r : r + 1] = jnp.sum(sums[r], 0, keepdims=True)
            vec_mate.start()
        weave(act_back(s, chain), beside)
    send_wide(0, 0)

    def rows_at(b, first, size):
        return pl.ds(pl.multiple_of(b * block_rows + first, 16), size)

    def first_copy(b, j):
        to = (col + j) % SIDE
        return remote(
            flat_b.at[rows_at(b, to * quarter, quarter)], rv1.at[b, j - 1],
            rs1_sem.at[b, j], dev(line * SIDE + to),
        )

    def second_copy(b, j):
        to = (line + j) % SIDE
        return remote(
            part_b.at[b, pl.ds(pl.multiple_of(to * piece, piece), piece)], rv2.at[b, j - 1],
            rs2_sem.at[b, j], dev(to * SIDE + col),
        )

    def other_copy(b, j):
        return remote(
            last.at[b], rvx.at[b, j - 1], rsx_sem.at[b, j], mid_dev((mid + j) % others)
        )

    def line_copy(b, j):
        span = res.at[core, rows_at(b, col * quarter + line * piece, piece)]
        return remote(span, span, ag2_sem.at[b, j], dev((line + j) % SIDE * SIDE + col))

    def col_copy(b, j):
        span = res.at[core, rows_at(b, col * quarter, quarter)]
        return remote(span, span, ag1_sem.at[b, j], dev(line * SIDE + (col + j) % SIDE))

    def mate_copy(b, j):
        at = (col + SIDE - j) % SIDE
        span = res.at[core, rows_at(b, at * quarter, quarter)]
        return remote(span, span, fwd_sem.at[b, j], mate)

    def vec_first(j):
        return remote(v1, rvv1.at[j - 1], vv1_sem.at[j], dev(line * SIDE + (col + j) % SIDE))

    def vec_second(j):
        return remote(v2, rvv2.at[j - 1], vv2_sem.at[j], dev((line + j) % SIDE * SIDE + col))

    def vec_other(j):
        return remote(v3, rvvx.at[j - 1], vvx_sem.at[j], mid_dev((mid + j) % others))

    peers = range(1, SIDE)

    def send_block(b):
        at = slice(b * block_rows, (b + 1) * block_rows)
        flat_b[at] = flat[at].astype(BF16)
        for j in peers:
            first_copy(b, j).start()

    def last_terms():
        weave(gather_grads([own_pair(0), mate_pair(0)], only=send_block))

    pl.when(core == 0)(last_terms)
    weave(drop_back(*order[-1]))
    join_chains(gs)
    tg_start()
    tg_o[own] = gs[own]
    pl.when(core == 1)(last_terms)
    vec_mate.wait_recv()
    v1[...] = v0[...] + rvm[...]
    for j in peers:
        vec_first(j).start()
    for b in range(blocks):
        for j in peers:
            first_copy(b, j).wait_recv()
        total = flat[rows_at(b, col * quarter, quarter)]
        for j in range(SIDE - 1):
            total = total + rv1[b, j].astype(F32)
        part[b] = total
        part_b[b] = total.astype(BF16)
        for j in peers:
            second_copy(b, j).start()
        if b == 0:
            for j in peers:
                vec_first(j).wait_recv()
            v2[...] = v1[...] + rvv1[0] + rvv1[1] + rvv1[2]
            for j in peers:
                vec_second(j).start()
    for b in range(blocks):
        for j in peers:
            second_copy(b, j).wait_recv()
        total = part[b, pl.ds(pl.multiple_of(line * piece, piece), piece)]
        for j in range(SIDE - 1):
            total = total + rv2[b, j].astype(F32)
        if others > 1:
            last[b] = total.astype(BF16)
            for j in range(1, others):
                other_copy(b, j).start()
            for j in range(1, others):
                other_copy(b, j).wait_recv()
                total = total + rvx[b, j - 1].astype(F32)
        res[core, rows_at(b, col * quarter + line * piece, piece)] = total.astype(BF16)
        for j in peers:
            line_copy(b, j).start()
    for j in peers:
        vec_second(j).wait_recv()
    vec = v2[...] + rvv2[0] + rvv2[1] + rvv2[2]
    if others > 1:
        v3[...] = vec
        for j in range(1, others):
            vec_other(j).start()
        for j in range(1, others):
            vec_other(j).wait_recv()
            vec = vec + rvvx[j - 1]
    vec_o[...] = vec
    for b in range(blocks):
        for j in peers:
            line_copy(b, j).wait_recv()
        for j in peers:
            col_copy(b, j).start()
        mate_copy(b, 0).start()
    for b in range(blocks):
        for j in peers:
            col_copy(b, j).wait_recv()
            mate_copy(b, j).start()

    tok_sent()
    og_sent()
    net_sent()
    tg_sent()
    for s in range(SECTIONS):
        for copy in mate_copies(s):
            copy.wait_send()
    vec_mate.wait_send()
    for j in peers:
        vec_first(j).wait_send()
        vec_second(j).wait_send()
        for b in range(blocks):
            for copy in (first_copy, second_copy, line_copy, col_copy):
                copy(b, j).wait_send()
    for j in range(1, others):
        vec_other(j).wait_send()
        for b in range(blocks):
            other_copy(b, j).wait_send()
    net_received()
    tg_received()
    for b in range(blocks):
        for j in range(SIDE):
            mate_copy(b, j).wait()


def finish_kernel(
    scale, res, net, tg, vec, gate, net_o, tg_o, spread_out, merge_out, bias_o, gate_o,
    spread_o, merge_o, sems,
):
    units = net.shape[1]
    tall, wide = spread_o.shape
    copies = []
    for c in range(wide // LANES):
        across = slice(c * LANES, (c + 1) * LANES)
        spread_o[:, across] = res[1, c * tall : (c + 1) * tall].astype(F32) * scale
        copies.append(
            pltpu.make_async_copy(
                spread_o.at[:, across], spread_out.at[:, across], sems.at[0, c]
            )
        )
        copies[-1].start()
    for c in range(wide // LANES):
        across = slice(c * LANES, (c + 1) * LANES)
        for k in range(tall // LANES):
            at = c * tall + k * LANES
            merge_o[across, k * LANES : (k + 1) * LANES] = (
                res[0, at : at + LANES].astype(F32) * scale
            ).T
        copies.append(
            pltpu.make_async_copy(merge_o.at[across], merge_out.at[across], sems.at[1, c])
        )
        copies[-1].start()
    net_o[...] = net[...].T
    tg_o[...] = tg[...].T
    opened = jax.nn.sigmoid(gate[...])
    opened = opened * (1.0 - opened) * scale
    both = [
        jnp.concatenate([vec[r : r + 1, :units], vec[r + 1 : r + 2, :units]], 1) for r in (0, 2)
    ]
    bias_o[...] = both[0].reshape(-1) * (0.25 * scale)
    gate_o[...] = both[1].reshape(-1) * opened
    for copy in copies:
        copy.wait()


def on_device(tokens, out_grad, spread_weight, merge_weight, switch_bias, gate_logit):
    n = lax.axis_size("seq")
    rows, units = tokens.shape
    switch, hidden_size = spread_weight.shape
    half = rows // 2
    wide_units = rounded_up(units)
    others = n // (2 * GROUP)
    more = max(others - 1, 1)
    flat_rows = switch * hidden_size // LANES
    blocks = hidden_size // (2 * LANES)
    quarter = flat_rows // (blocks * SIDE)
    piece = quarter // SIDE
    vec_shape = (4, wide_units)
    any_spec = pl.BlockSpec(memory_space=pltpu.HBM)
    vmem_spec = pl.BlockSpec(memory_space=pltpu.VMEM)
    dma = pltpu.SemaphoreType.DMA
    vmem = pltpu.VMEM
    net, tg, res, vec = pl.pallas_call(
        functools.partial(step_kernel, n),
        out_shape=(
            jax.ShapeDtypeStruct((rows, units), BF16),
            jax.ShapeDtypeStruct((rows, units), BF16),
            jax.ShapeDtypeStruct((2, flat_rows, LANES), BF16),
            jax.ShapeDtypeStruct(vec_shape, F32),
        ),
        in_specs=[any_spec] * 6,
        out_specs=(vmem_spec,) * 4,
        scratch_shapes=[
            vmem((switch, hidden_size), BF16),
            vmem((hidden_size, switch), BF16),
            vmem((switch,), F32),
            vmem((switch,), F32),
            vmem((units, rows), BF16),
            vmem((units, rows), BF16),
            vmem((rows, units), BF16),
            vmem((rows, units), BF16),
            vmem((rows, units), BF16),
            vmem((rows, units), BF16),
            vmem((rows, units), BF16),
            vmem((rows, units), BF16),
            vmem((rows, wide_units), BF16),
            vmem((2, wide_units, hidden_size), BF16),
            vmem((2, hidden_size, wide_units), BF16),
            vmem((2, hidden_size, wide_units), BF16),
            vmem((2, wide_units, hidden_size), BF16),
            vmem((8, wide_units), F32),
            vmem((2, SECTIONS, 2, half, wide_units), BF16),
            vmem((2, SECTIONS, half, hidden_size), BF16),
            vmem((SECTIONS, 2, half, wide_units), BF16),
            vmem((SECTIONS, half, hidden_size), BF16),
            vmem((half, hidden_size), F32),
            vmem((SECTIONS, half, hidden_size), F32),
            vmem((SECTIONS, half, hidden_size), F32),
            vmem((SECTIONS, half, LANES), F32),
            vmem((flat_rows, LANES), F32),
            vmem((flat_rows, LANES), BF16),
            vmem((blocks, quarter, LANES), F32),
            vmem((blocks, quarter, LANES), BF16),
            vmem((blocks, SIDE - 1, quarter, LANES), BF16),
            vmem((blocks, SIDE - 1, piece, LANES), BF16),
            vmem((blocks, more, piece, LANES), BF16),
            vmem((blocks, piece, LANES), BF16),
            vmem((4, 8, wide_units), F32),
            vmem(vec_shape, F32),
            vmem(vec_shape, F32),
            vmem(vec_shape, F32),
            vmem(vec_shape, F32),
            vmem(vec_shape, F32),
            vmem((SIDE - 1,) + vec_shape, F32),
            vmem((SIDE - 1,) + vec_shape, F32),
            vmem((more,) + vec_shape, F32),
            dma((6,)),
            dma((4, GROUP, 2)),
            dma((2, SECTIONS, 2)),
            dma((blocks, SIDE, 2)),
            dma((blocks, SIDE, 2)),
            dma((blocks, more + 1, 2)),
            dma((blocks, SIDE, 2)),
            dma((blocks, SIDE, 2)),
            dma((blocks, SIDE, 2)),
            dma((2,)),
            dma((SIDE, 2)),
            dma((SIDE, 2)),
            dma((more + 1, 2)),
        ],
        compiler_params=pltpu.CompilerParams(
            collective_id=0, has_side_effects=True, vmem_limit_bytes=61 * 2**20
        ),
        name="switch_step",
    )(tokens.T, out_grad.T, spread_weight, merge_weight, switch_bias, gate_logit)
    scale = 1.0 / math.sqrt(n * rows)
    net, tg, spread, merge, bias, gate = pl.pallas_call(
        functools.partial(finish_kernel, scale),
        out_shape=(
            jax.ShapeDtypeStruct((units, rows), BF16),
            jax.ShapeDtypeStruct((units, rows), BF16),
            jax.ShapeDtypeStruct((switch, hidden_size), F32),
            jax.ShapeDtypeStruct((hidden_size, switch), F32),
            jax.ShapeDtypeStruct((switch,), F32),
            jax.ShapeDtypeStruct((switch,), F32),
        ),
        in_specs=[vmem_spec] * 5,
        out_specs=(vmem_spec, vmem_spec, any_spec, any_spec, vmem_spec, vmem_spec),
        scratch_shapes=[
            vmem((switch, hidden_size), F32),
            vmem((hidden_size, switch), F32),
            dma((2, hidden_size // LANES)),
        ],
        compiler_params=pltpu.CompilerParams(vmem_limit_bytes=61 * 2**20),
        name="finish",
    )(res, net, tg, vec, gate_logit)
    return net.T, tg.T, spread, merge, bias, gate


def solution(mesh):
    placed = (P("seq", None), P("seq", None), P(), P(), P(), P())
    return jax.shard_map(
        on_device,
        mesh=mesh,
        in_specs=placed,
        out_specs=placed,
        check_vma=False,
    )
```

```python
import functools
import math

import jax
import jax.numpy as jnp
from jax import lax
from jax.experimental import pallas as pl
from jax.experimental.pallas import tpu as pltpu
from jax.sharding import PartitionSpec as P

SECTIONS = 4
GROUP = 2**SECTIONS
SIDE = 4
LANES = 128
MESH = pl.DeviceIdType.MESH
F32 = jnp.float32
BF16 = jnp.bfloat16

log2_e = 1.4426950408889634
inv_sqrt_two_pi = 0.3989422804014327


def dot(a, b):
    return jnp.dot(a, b, preferred_element_type=F32)


def distribution(value, bell):
    base = 1.0 + (0.3275911 * 0.7071067811865476) * jnp.abs(value)
    guess = pl.reciprocal(base, approx=True)
    t = guess * (2.0 - base * guess)
    tail = 0.5 * 1.061405429
    for factor in (-1.453152027, 1.421413741, -0.284496736, 0.254829592):
        tail = tail * t + 0.5 * factor
    tail = tail * t * bell
    return jnp.where(value < 0.0, tail, 1.0 - tail)


def weave(*tasks):
    steps = [
        ((k + 0.5) / len(task), number, step)
        for number, task in enumerate(tasks)
        for k, step in enumerate(task)
    ]
    for _, _, step in sorted(steps, key=lambda entry: entry[:2]):
        step()


def rounded_up(size):
    return -(-size // LANES) * LANES


def step_kernel(
    n,
    tok, og, sw, mw, bias, gate,
    net_o, tg_o, res, vec_o,
    sw_v, mw_v, bias_v, gate_v,
    xt, gt, tok_v, og_v, xin, gin, xs, gs,
    state, wp, wt, mp, mt, rows_v,
    sides, wides, r_sides, r_wides,
    pre, normed, slope, inv,
    flat, flat_b, part, part_b, rv1, rv2, rvx, last,
    sums, v0, v1, v2, v3, rvm, rvv1, rvv2, rvvx,
    load_sem, a2a_sem, mate_sem, rs1_sem, rs2_sem, rsx_sem, ag1_sem, ag2_sem, fwd_sem,
    vm_sem, vv1_sem, vv2_sem, vvx_sem,
):
    rows, units = xin.shape
    sub = rows // GROUP
    half = rows // 2
    hidden_size = sw_v.shape[1]
    stride = n // GROUP
    others = n // (2 * GROUP)
    blocks = rv1.shape[0]
    block_rows = flat.shape[0] // blocks
    quarter = block_rows // SIDE
    piece = quarter // SIDE

    me = lax.axis_index("seq")
    top = me // stride
    low = me % stride
    core = me % 2
    mid = low // 2
    mate = me + 1 - 2 * core
    col = top % SIDE
    line = top // SIDE

    def dev(which):
        return which * stride + low

    def mid_dev(which):
        return top * stride + which * 2 + core

    def remote(src, dst, sems, target):
        return pltpu.make_async_remote_copy(
            src_ref=src, dst_ref=dst, send_sem=sems.at[0], recv_sem=sems.at[1],
            device_id=(target,), device_id_type=MESH,
        )

    loads = [
        pltpu.make_async_copy(tok, xt, load_sem.at[0]),
        pltpu.make_async_copy(og, gt, load_sem.at[1]),
        pltpu.make_async_copy(sw, sw_v, load_sem.at[2]),
        pltpu.make_async_copy(mw, mw_v, load_sem.at[3]),
        pltpu.make_async_copy(bias, bias_v, load_sem.at[4]),
        pltpu.make_async_copy(gate, gate_v, load_sem.at[5]),
    ]
    for load in loads:
        load.start()

    barrier = pltpu.get_barrier_semaphore()

    @pl.loop(1, GROUP)
    def _(j):
        pl.semaphore_signal(barrier, inc=1, device_id=(dev((top + j) % GROUP),), device_id_type=MESH)

    pl.semaphore_signal(barrier, inc=1, device_id=(mate,), device_id_type=MESH)
    for j in range(1, others):
        pl.semaphore_signal(
            barrier, inc=1, device_id=(mid_dev((mid + j) % others),), device_id_type=MESH
        )
    own = pl.ds(pl.multiple_of(top * sub, sub), sub)
    loads[0].wait()
    tok_v[...] = xt[...].T
    xin[own] = tok_v[own]
    pl.semaphore_wait(barrier, GROUP + others - 1)

    def exchange(src, dst, number):
        def one(j):
            to = (top + j) % GROUP
            return remote(
                src.at[pl.ds(to * sub, sub)], dst.at[pl.ds(top * sub, sub)],
                a2a_sem.at[number, j], dev(to),
            )

        def start():
            @pl.loop(1, GROUP)
            def _(j):
                one(j).start()

        def received():
            @pl.loop(1, GROUP)
            def _(j):
                one(j).wait_recv()

        def sent():
            @pl.loop(1, GROUP)
            def _(j):
                one(j).wait_send()

        return start, received, sent

    tok_start, tok_received, tok_sent = exchange(tok_v, xin, 0)
    og_start, og_received, og_sent = exchange(og_v, gin, 1)
    net_start, net_received, net_sent = exchange(xs, net_o, 2)
    tg_start, tg_received, tg_sent = exchange(gs, tg_o, 3)
    tok_start()
    loads[1].wait()
    og_v[...] = gt[...].T
    gin[own] = og_v[own]

    pad = wp.shape[1] - units
    loads[2].wait()
    loads[3].wait()
    turned = mw_v[...].T
    for h in range(2):
        wp[h, :units] = sw_v[h * units : (h + 1) * units]
        wp[h, units:] = jnp.zeros((pad, hidden_size), BF16)
        wt[h] = wp[h].T
        mt[h, :units] = turned[h * units : (h + 1) * units]
        mt[h, units:] = jnp.zeros((pad, hidden_size), BF16)
        mp[h] = mt[h].T
    loads[4].wait()
    loads[5].wait()
    rows_v[...] = jnp.zeros(rows_v.shape, F32)
    for h in range(2):
        rows_v[h : h + 1, :units] = jax.nn.sigmoid(gate_v[...].reshape(1, -1)[:, h * units : (h + 1) * units])
        rows_v[2 + h : 3 + h, :units] = bias_v[...].reshape(1, -1)[:, h * units : (h + 1) * units]
    sums[...] = jnp.zeros(sums.shape, F32)
    state[...] = jnp.zeros(state.shape, BF16)

    chains = 2
    chain_rows = half // chains
    part_rows = sub // chains
    chunk = 16
    width = hidden_size // blocks

    def spans(section, chain):
        length = chain_rows >> section
        for k in range(2**section):
            for h in range(2):
                at = chain * rows // chains + (2 * k + h) * length
                inner = chain * chain_rows + k * length
                yield h, slice(inner, inner + length), slice(at, at + length)

    def rows_of(chain):
        return slice(chain * chain_rows, (chain + 1) * chain_rows)

    def split_chains(source):
        for chain in range(chains):
            for b in range(GROUP):
                at = (chain * GROUP + b) * part_rows
                start = b * sub + chain * part_rows
                state[at : at + part_rows, :units] = source[start : start + part_rows]

    def join_chains(target):
        for chain in range(chains):
            for b in range(GROUP):
                at = (chain * GROUP + b) * part_rows
                start = b * sub + chain * part_rows
                target[start : start + part_rows] = state[at : at + part_rows, :units]

    def products(left, weights, at):
        def one(b):
            cols = slice(b * width, (b + 1) * width)
            pre[at, cols] = dot(left[0, at], weights[0, :, cols]) + dot(
                left[1, at], weights[1, :, cols]
            )

        return [functools.partial(one, b) for b in range(blocks)]

    def lift(s, chain):
        def pairs():
            for h, inner, outer in spans(s, chain):
                sides[1, s, h, inner] = state[outer]

        return [pairs] + products(sides.at[1, s], wp, rows_of(chain))

    def act(s, chain):
        def one(i):
            at = slice(chain * chain_rows + i * chunk, chain * chain_rows + (i + 1) * chunk)
            value = pre[at]
            centered = value - jnp.mean(value, -1, keepdims=True)
            scale = lax.rsqrt(jnp.mean(centered * centered, -1, keepdims=True) + 1e-05)
            value = centered * scale
            bell = jnp.exp2(value * value * (-0.5 * log2_e))
            phi_sum = distribution(value, bell)
            wides[0, s, at] = (value * phi_sum).astype(BF16)
            normed[s, at] = value
            slope[s, at] = phi_sum + value * bell * inv_sqrt_two_pi
            inv[s, at] = jnp.broadcast_to(scale, (chunk, LANES))

        return [functools.partial(one, i) for i in range(chain_rows // chunk)]

    def drop(s, chain):
        at = rows_of(chain)

        def one(h):
            out = (
                rows_v[h : h + 1] * sides[1, s, h, at].astype(F32)
                + 0.25 * (dot(wides[0, s, at], mp[h]) + rows_v[2 + h : 3 + h])
            ).astype(BF16)
            for side, inner, outer in spans(s, chain):
                if side == h:
                    start = inner.start - at.start
                    state[outer] = out[start : start + inner.stop - inner.start]

        return [functools.partial(one, h) for h in range(2)]

    def lift_back(s, chain):
        at = rows_of(chain)

        def pairs():
            for h, inner, outer in spans(s, chain):
                sides[0, s, h, inner] = (0.25 * state[outer].astype(F32)).astype(BF16)

        def add_up():
            for h in range(2):
                value = 4.0 * sides[0, s, h, at].astype(F32)
                gated = value * sides[1, s, h, at].astype(F32)
                sums[h] += jnp.sum(value.reshape(-1, 8, value.shape[1]), 0)
                sums[2 + h] += jnp.sum(gated.reshape(-1, 8, value.shape[1]), 0)

        return [pairs] + products(sides.at[0, s], mt, at) + [add_up]

    def act_back(s, chain):
        def one(i):
            at = slice(chain * chain_rows + i * chunk, chain * chain_rows + (i + 1) * chunk)
            value = normed[s, at]
            grad = pre[at] * slope[s, at]
            grad = (
                grad
                - jnp.mean(grad, -1, keepdims=True)
                - value * jnp.mean(grad * value, -1, keepdims=True)
            ) * inv[s, at][:, :1]
            wides[1, s, at] = grad.astype(BF16)

        return [functools.partial(one, i) for i in range(chain_rows // chunk)]

    def drop_back(s, chain):
        at = rows_of(chain)

        def one(h):
            back = dot(wides[1, s, at], wt[h])
            for side, inner, outer in spans(s, chain):
                if side == h:
                    start = inner.start - at.start
                    state[outer] = (
                        rows_v[h : h + 1] * state[outer].astype(F32)
                        + back[start : start + inner.stop - inner.start]
                    ).astype(BF16)

        return [functools.partial(one, h) for h in range(2)]

    tok_received()
    og_start()
    split_chains(xin)
    order = [(s, chain) for s in range(SECTIONS) for chain in range(chains)]
    weave(lift(*order[0]))
    for k, phase in enumerate(order):
        beside = drop(*order[k - 1]) if k else []
        if k + 1 < len(order):
            beside += lift(*order[k + 1])
        weave(act(*phase), beside)
    weave(drop(*order[-1]))
    join_chains(xs)
    net_start()
    net_o[own] = xs[own]

    def gather_grads(pairs, first=False, only=None):
        turned = {}

        def turn(k, h):
            turned[k, h] = pairs[k][0][h].T[:units]

        def one(b, h):
            term = sum(
                dot(turned[k, h], wide[:, b * width : (b + 1) * width])
                for k, (_, wide) in enumerate(pairs)
            )
            for c in range(width // LANES):
                at = b * block_rows + (2 * c + h) * units
                at = slice(at, at + units)
                block = term[:, c * LANES : (c + 1) * LANES]
                block = block if first else flat[at] + block
                flat[at] = block
                if only is not None:
                    flat_b[at] = block.astype(BF16)
            if only is not None and h == 1:
                only(b)

        steps = [functools.partial(turn, k, h) for k in range(len(pairs)) for h in range(2)]
        return steps + [functools.partial(one, b, h) for b in range(blocks) for h in range(2)]

    def mate_copies(s):
        return [
            remote(sides.at[1 - core, s], r_sides.at[s], mate_sem.at[0, s], mate),
            remote(wides.at[1 - core, s], r_wides.at[s], mate_sem.at[1, s], mate),
        ]

    vec_mate = remote(v0, rvm, vm_sem, mate)
    og_received()
    split_chains(gin)

    def own_pair(s):
        return sides.at[core, s], wides.at[core, s]

    def mate_pair(s):
        for copy in mate_copies(s):
            copy.wait_recv()
        return r_sides.at[s], r_wides.at[s]

    def send_wide(s, sender):
        @pl.when(core == sender)
        def _():
            mate_copies(s)[1].start()

    order = [(s, chain) for s in reversed(range(SECTIONS)) for chain in range(chains)]
    weave(lift_back(*order[0]))
    for k, (s, chain) in enumerate(order):
        beside = drop_back(*order[k - 1]) if k else []
        if chain == 0 and s < SECTIONS - 1:
            send_wide(s + 1, 0)
            pairs = [own_pair(s + 1)]
            if s < SECTIONS - 2:
                pairs.append(mate_pair(s + 2))
            beside += gather_grads(pairs, s == SECTIONS - 2)
        if chain == 1:
            mate_copies(s)[0].start()
            send_wide(s, 1)
        if (s, chain) == (0, 1):
            beside += gather_grads([mate_pair(1)])
        if k + 1 < len(order):
            beside += lift_back(*order[k + 1])
        else:
            for r in range(4):
                v0[r : r + 1] = jnp.sum(sums[r], 0, keepdims=True)
            vec_mate.start()
        weave(act_back(s, chain), beside)
    send_wide(0, 0)
    weave(drop_back(*order[-1]), gather_grads([own_pair(0)]))
    join_chains(gs)
    tg_start()
    tg_o[own] = gs[own]

    def rows_at(b, first, size):
        return pl.ds(pl.multiple_of(b * block_rows + first, 16), size)

    def first_copy(b, j):
        to = (col + j) % SIDE
        return remote(
            flat_b.at[rows_at(b, to * quarter, quarter)], rv1.at[b, j - 1],
            rs1_sem.at[b, j], dev(line * SIDE + to),
        )

    def second_copy(b, j):
        to = (line + j) % SIDE
        return remote(
            part_b.at[b, pl.ds(pl.multiple_of(to * piece, piece), piece)], rv2.at[b, j - 1],
            rs2_sem.at[b, j], dev(to * SIDE + col),
        )

    def other_copy(b, j):
        return remote(
            last.at[b], rvx.at[b, j - 1], rsx_sem.at[b, j], mid_dev((mid + j) % others)
        )

    def line_copy(b, j):
        span = res.at[core, rows_at(b, col * quarter + line * piece, piece)]
        return remote(span, span, ag2_sem.at[b, j], dev((line + j) % SIDE * SIDE + col))

    def col_copy(b, j):
        span = res.at[core, rows_at(b, col * quarter, quarter)]
        return remote(span, span, ag1_sem.at[b, j], dev(line * SIDE + (col + j) % SIDE))

    def mate_copy(b, j):
        at = (col + SIDE - j) % SIDE
        span = res.at[core, rows_at(b, at * quarter, quarter)]
        return remote(span, span, fwd_sem.at[b, j], mate)

    def vec_first(j):
        return remote(v1, rvv1.at[j - 1], vv1_sem.at[j], dev(line * SIDE + (col + j) % SIDE))

    def vec_second(j):
        return remote(v2, rvv2.at[j - 1], vv2_sem.at[j], dev((line + j) % SIDE * SIDE + col))

    def vec_other(j):
        return remote(v3, rvvx.at[j - 1], vvx_sem.at[j], mid_dev((mid + j) % others))

    peers = range(1, SIDE)

    def send_block(b):
        for j in peers:
            first_copy(b, j).start()

    vec_mate.wait_recv()
    v1[...] = v0[...] + rvm[...]
    for j in peers:
        vec_first(j).start()
    mate_copies(0)[0].wait_recv()
    final = gather_grads([(r_sides.at[0], r_wides.at[0])], only=send_block)
    weave(final[:2])
    mate_copies(0)[1].wait_recv()
    weave(final[2:])
    for b in range(blocks):
        for j in peers:
            first_copy(b, j).wait_recv()
        total = flat[rows_at(b, col * quarter, quarter)]
        for j in range(SIDE - 1):
            total = total + rv1[b, j].astype(F32)
        part[b] = total
        part_b[b] = total.astype(BF16)
        for j in peers:
            second_copy(b, j).start()
        if b == 0:
            for j in peers:
                vec_first(j).wait_recv()
            v2[...] = v1[...] + rvv1[0] + rvv1[1] + rvv1[2]
            for j in peers:
                vec_second(j).start()
    for b in range(blocks):
        for j in peers:
            second_copy(b, j).wait_recv()
        total = part[b, pl.ds(pl.multiple_of(line * piece, piece), piece)]
        for j in range(SIDE - 1):
            total = total + rv2[b, j].astype(F32)
        if others > 1:
            last[b] = total.astype(BF16)
            for j in range(1, others):
                other_copy(b, j).start()
            for j in range(1, others):
                other_copy(b, j).wait_recv()
                total = total + rvx[b, j - 1].astype(F32)
        res[core, rows_at(b, col * quarter + line * piece, piece)] = total.astype(BF16)
        for j in peers:
            line_copy(b, j).start()
    for j in peers:
        vec_second(j).wait_recv()
    vec = v2[...] + rvv2[0] + rvv2[1] + rvv2[2]
    if others > 1:
        v3[...] = vec
        for j in range(1, others):
            vec_other(j).start()
        for j in range(1, others):
            vec_other(j).wait_recv()
            vec = vec + rvvx[j - 1]
    vec_o[...] = vec
    for b in range(blocks):
        for j in peers:
            line_copy(b, j).wait_recv()
        for j in peers:
            col_copy(b, j).start()
        mate_copy(b, 0).start()
    for b in range(blocks):
        for j in peers:
            col_copy(b, j).wait_recv()
            mate_copy(b, j).start()

    tok_sent()
    og_sent()
    net_sent()
    tg_sent()
    for s in range(SECTIONS):
        for copy in mate_copies(s):
            copy.wait_send()
    vec_mate.wait_send()
    for j in peers:
        vec_first(j).wait_send()
        vec_second(j).wait_send()
        for b in range(blocks):
            for copy in (first_copy, second_copy, line_copy, col_copy):
                copy(b, j).wait_send()
    for j in range(1, others):
        vec_other(j).wait_send()
        for b in range(blocks):
            other_copy(b, j).wait_send()
    net_received()
    tg_received()
    for b in range(blocks):
        for j in range(SIDE):
            mate_copy(b, j).wait()


def finish_kernel(scale, res, net, tg, vec, gate, net_o, tg_o, spread_o, merge_o, bias_o, gate_o):
    units = net.shape[1]
    tall, wide = spread_o.shape
    net_o[...] = net[...].T
    tg_o[...] = tg[...].T
    for c in range(wide // LANES):
        across = slice(c * LANES, (c + 1) * LANES)
        spread_o[:, across] = res[1, c * tall : (c + 1) * tall].astype(F32) * scale
        for k in range(tall // LANES):
            at = c * tall + k * LANES
            merge_o[across, k * LANES : (k + 1) * LANES] = (
                res[0, at : at + LANES].astype(F32) * scale
            ).T
    opened = jax.nn.sigmoid(gate[...])
    opened = opened * (1.0 - opened) * scale
    both = [
        jnp.concatenate([vec[r : r + 1, :units], vec[r + 1 : r + 2, :units]], 1) for r in (0, 2)
    ]
    bias_o[...] = both[0].reshape(-1) * (0.25 * scale)
    gate_o[...] = both[1].reshape(-1) * opened


def on_device(tokens, out_grad, spread_weight, merge_weight, switch_bias, gate_logit):
    n = lax.axis_size("seq")
    rows, units = tokens.shape
    switch, hidden_size = spread_weight.shape
    half = rows // 2
    wide_units = rounded_up(units)
    others = n // (2 * GROUP)
    more = max(others - 1, 1)
    flat_rows = switch * hidden_size // LANES
    blocks = hidden_size // (2 * LANES)
    quarter = flat_rows // (blocks * SIDE)
    piece = quarter // SIDE
    vec_shape = (4, wide_units)
    any_spec = pl.BlockSpec(memory_space=pltpu.HBM)
    vmem_spec = pl.BlockSpec(memory_space=pltpu.VMEM)
    dma = pltpu.SemaphoreType.DMA
    vmem = pltpu.VMEM
    net, tg, res, vec = pl.pallas_call(
        functools.partial(step_kernel, n),
        out_shape=(
            jax.ShapeDtypeStruct((rows, units), BF16),
            jax.ShapeDtypeStruct((rows, units), BF16),
            jax.ShapeDtypeStruct((2, flat_rows, LANES), BF16),
            jax.ShapeDtypeStruct(vec_shape, F32),
        ),
        in_specs=[any_spec] * 6,
        out_specs=(vmem_spec,) * 4,
        scratch_shapes=[
            vmem((switch, hidden_size), BF16),
            vmem((hidden_size, switch), BF16),
            vmem((switch,), F32),
            vmem((switch,), F32),
            vmem((units, rows), BF16),
            vmem((units, rows), BF16),
            vmem((rows, units), BF16),
            vmem((rows, units), BF16),
            vmem((rows, units), BF16),
            vmem((rows, units), BF16),
            vmem((rows, units), BF16),
            vmem((rows, units), BF16),
            vmem((rows, wide_units), BF16),
            vmem((2, wide_units, hidden_size), BF16),
            vmem((2, hidden_size, wide_units), BF16),
            vmem((2, hidden_size, wide_units), BF16),
            vmem((2, wide_units, hidden_size), BF16),
            vmem((8, wide_units), F32),
            vmem((2, SECTIONS, 2, half, wide_units), BF16),
            vmem((2, SECTIONS, half, hidden_size), BF16),
            vmem((SECTIONS, 2, half, wide_units), BF16),
            vmem((SECTIONS, half, hidden_size), BF16),
            vmem((half, hidden_size), F32),
            vmem((SECTIONS, half, hidden_size), F32),
            vmem((SECTIONS, half, hidden_size), F32),
            vmem((SECTIONS, half, LANES), F32),
            vmem((flat_rows, LANES), F32),
            vmem((flat_rows, LANES), BF16),
            vmem((blocks, quarter, LANES), F32),
            vmem((blocks, quarter, LANES), BF16),
            vmem((blocks, SIDE - 1, quarter, LANES), BF16),
            vmem((blocks, SIDE - 1, piece, LANES), BF16),
            vmem((blocks, more, piece, LANES), BF16),
            vmem((blocks, piece, LANES), BF16),
            vmem((4, 8, wide_units), F32),
            vmem(vec_shape, F32),
            vmem(vec_shape, F32),
            vmem(vec_shape, F32),
            vmem(vec_shape, F32),
            vmem(vec_shape, F32),
            vmem((SIDE - 1,) + vec_shape, F32),
            vmem((SIDE - 1,) + vec_shape, F32),
            vmem((more,) + vec_shape, F32),
            dma((6,)),
            dma((4, GROUP, 2)),
            dma((2, SECTIONS, 2)),
            dma((blocks, SIDE, 2)),
            dma((blocks, SIDE, 2)),
            dma((blocks, more + 1, 2)),
            dma((blocks, SIDE, 2)),
            dma((blocks, SIDE, 2)),
            dma((blocks, SIDE, 2)),
            dma((2,)),
            dma((SIDE, 2)),
            dma((SIDE, 2)),
            dma((more + 1, 2)),
        ],
        compiler_params=pltpu.CompilerParams(
            collective_id=0, has_side_effects=True, vmem_limit_bytes=61 * 2**20
        ),
        name="switch_step",
    )(tokens.T, out_grad.T, spread_weight, merge_weight, switch_bias, gate_logit)
    scale = 1.0 / math.sqrt(n * rows)
    net, tg, spread, merge, bias, gate = pl.pallas_call(
        functools.partial(finish_kernel, scale),
        out_shape=(
            jax.ShapeDtypeStruct((units, rows), BF16),
            jax.ShapeDtypeStruct((units, rows), BF16),
            jax.ShapeDtypeStruct((switch, hidden_size), F32),
            jax.ShapeDtypeStruct((hidden_size, switch), F32),
            jax.ShapeDtypeStruct((switch,), F32),
            jax.ShapeDtypeStruct((switch,), F32),
        ),
        in_specs=[vmem_spec] * 5,
        out_specs=(vmem_spec,) * 6,
        compiler_params=pltpu.CompilerParams(vmem_limit_bytes=61 * 2**20),
        name="finish",
    )(res, net, tg, vec, gate_logit)
    return net.T, tg.T, spread, merge, bias, gate


def solution(mesh):
    placed = (P("seq", None), P("seq", None), P(), P(), P(), P())
    return jax.shard_map(
        on_device,
        mesh=mesh,
        in_specs=placed,
        out_specs=placed,
        check_vma=False,
    )
```
